256 devices in a mesh: pos: 4 (over y), vocab: 64 (over z, x, core).
Axes of the slice: x: 4, y: 4, z: 8, core: 2. Of those that a mesh axis runs over, the one named last changes fastest.
Arguments:
- quantized: bfloat16 [64, 5, 8, 4096], P('vocab', None, 'pos'), may hold values from -17 to 17
- scales: float32 [64, 5, 8, 32], P('vocab', None, 'pos'), may hold values from 0.25 to 4
- norm_gain: float32 [4096], replicated, may hold values from 0.25 to 1.75
- embed_table: bfloat16 [81920, 4096], P('vocab'), may hold values from -0.390625 to 0.390625
- counts: int32 [8], replicated, may hold values from 1 to 320, 1024 in all
- positions: int32 [64, 5, 8], P(None, None, 'pos'), may hold values from 0 to 639, as said below
Outputs:
- expected: bfloat16 [64, 5, 8, 4096], P('vocab', None, 'pos')
- margins: float32 [8, 640], P('pos', 'vocab')
The draws below stay inside these ranges and needn't reach their ends.
Inputs may be any that keep to these rules, and one draw needn't show every extreme that they name: The counts of the 8 sequences sum to 1024; the largest is 320. Within each sequence the positions of its slots are distinct and rise with the slot number j = r * 64 + v.
All inputs are finite; a program needn't handle non-finite values.
Results may differ from the reference program's by a relative error of at most 0.011.
Values may be sent and summed in bfloat16 or wider, within the bound.
A program may use at most 128 MiB of HBM per device.

```python
import math
import jax
import jax.numpy as jnp
import numpy as np
from jax import lax

D = 4096
VOCAB = 81920
SEQS = 8
CD = 5
SLOT_COLS = 64
CAP = 320
MASKED = 1024
LEN = 640


def draw_quantized(key, part):
    key = jax.random.fold_in(key, 1)
    noise_key = jax.random.fold_in(key, 0)
    array_shape = (SLOT_COLS, CD, SEQS, D)
    values = jnp.clip(jax.random.normal(noise_key, array_shape, jnp.float32), -4.0, 4.0)
    return values.astype(jnp.bfloat16)


def draw_embed_table(key, part):
    key = jax.random.fold_in(key, 2)
    spread = 3.5 / math.sqrt(D)
    values = jnp.clip(jax.random.normal(key, (VOCAB, D), jnp.float32), -4.0, 4.0) * spread
    return values.astype(jnp.bfloat16)


def draw_positions(key, part):
    key = jax.random.fold_in(key, 3)

    def one_sequence(seq_key):
        inner = jax.random.permutation(seq_key, LEN - 2)[:CAP - 2].astype(jnp.int32) + 1
        return jnp.concatenate([jnp.zeros((1,), jnp.int32), jnp.sort(inner), jnp.full((1,), LEN - 1, jnp.int32)])
    rows_all = jax.vmap(one_sequence)(jax.random.split(key, SEQS))
    return rows_all.reshape(SEQS, CD, SLOT_COLS).transpose(2, 1, 0)


def shard_levels(key, dims, pieces, low, high):
    level, own = 1.0, jax.random.fold_in(key, 6)
    for axis_at, blocks in pieces:
        draws = jnp.exp(jax.random.uniform(jax.random.fold_in(own, axis_at), (blocks,), jnp.float32, low / len(pieces), high / len(pieces)))
        level = level * jnp.repeat(draws, dims[axis_at] // blocks).reshape([-1 if axis == axis_at else 1 for axis in range(len(dims))])
    return level


def profile(number_of, total, bound, lean):
    weights = [(1 << 20) // math.isqrt(grade ** lean) + 1 for grade in range(2, number_of + 1)]
    surplus, given = total - bound - (number_of - 1), [1] * (number_of - 1)
    while surplus > 0:
        movable = [i for i in range(number_of - 1) if given[i] < bound]
        pool, left = sum([weights[i] for i in movable]), surplus
        for i in movable:
            more = min(bound - given[i], max(1, left * weights[i] // pool), surplus)
            given[i] = given[i] + more
            surplus = surplus - more
    return np.array([bound] + given)


def ragged(key, amount, total, bound, skew):
    if amount == 2:
        one = jax.random.randint(key, (), max(1, total - bound), min(bound, total - 1) + 1)
        return jnp.stack([one, total - one])
    sizes = jnp.asarray(profile(amount, total, bound, skew), jnp.int32)
    couples = (amount - 1) // 2
    donor, taker = sizes[1:1 + 2 * couples:2], sizes[2:2 + 2 * couples:2]
    margin = jnp.minimum(donor - 1, bound - taker)
    moved = jax.random.randint(jax.random.fold_in(key, 1), (couples,), 0, 1 << 20) % (margin + 1)
    sizes = sizes.at[1:1 + 2 * couples:2].set(donor - moved).at[2:2 + 2 * couples:2].set(taker + moved)
    return sizes[jax.random.permutation(jax.random.fold_in(key, 2), amount)]


def setup_inputs(seed: int = 0) -> dict:
    seeds = jax.random.split(jax.random.key(seed), 7)
    return {
        "quantized": draw_quantized(jax.random.fold_in(seeds[6], 71), 0),
        "scales": jnp.clip(jnp.exp(math.log(4.0) - 2.7725887 * jax.random.uniform(seeds[1], (SLOT_COLS, CD, SEQS, D // 128), jnp.float32) ** shard_levels(seeds[1], (SLOT_COLS, CD, SEQS, D // 128), ((0, 64), (2, 4)), -0.2, 0.2)), 0.25, 4.0),
        "norm_gain": jnp.clip(1.0 + 0.15 * jax.random.normal(seeds[2], (D,), jnp.float32), 0.25, 1.75),
        "embed_table": draw_embed_table(jax.random.fold_in(seeds[6], 71), 0),
        "counts": ragged(seeds[4], SEQS, MASKED, CAP, 2).astype(jnp.int32),
        "positions": draw_positions(jax.random.fold_in(seeds[6], 71), 0),
    }


def readout_block(row_block, embed_table):
    logits = jnp.dot(row_block, embed_table.T, preferred_element_type=jnp.float32)
    leading = lax.top_k(logits, 2)[0]
    top_one = leading[:, 0]
    top_two = leading[:, 1]
    shifted = jnp.exp(logits - top_one[:, None])
    softmax_sum = lax.optimization_barrier(jnp.sum(shifted, axis=1))
    weights_soft = (shifted / softmax_sum[:, None]).astype(jnp.bfloat16)
    mixture = jnp.dot(weights_soft, embed_table, preferred_element_type=jnp.float32)
    mixture = (mixture * math.sqrt(D)).astype(jnp.bfloat16)
    margin_rows = (1.0 - jnp.exp(top_two - top_one)) / softmax_sum
    return (mixture, margin_rows)

def reference(quantized, scales, norm_gain, embed_table, counts, positions):
    column = jnp.arange(SLOT_COLS, dtype=jnp.int32)[:, None, None]
    row_id = jnp.arange(CD, dtype=jnp.int32)[None, :, None]
    live_mask = row_id * SLOT_COLS + column < counts[None, None, :]
    picked = jnp.nonzero(live_mask.reshape(-1), size=MASKED)[0].astype(jnp.int32)
    dequant = quantized.astype(jnp.float32).reshape(SLOT_COLS, CD, SEQS, D // 128, 128) * scales[..., None]
    dequant = dequant.reshape(-1, D)[picked]
    square_mean = lax.optimization_barrier(jnp.mean(dequant * dequant, axis=1, keepdims=True))
    normed = (dequant * lax.rsqrt(square_mean + 1e-06) * norm_gain).astype(jnp.bfloat16)
    blocks = normed.reshape(MASKED // 128, 128, D)
    mixture, margin_rows = lax.map(lambda row_block: readout_block(row_block, embed_table), blocks)
    expected = jnp.zeros((SLOT_COLS * CD * SEQS, D), jnp.bfloat16).at[picked].set(mixture.reshape(MASKED, D))
    seq_ids = (jnp.arange(SLOT_COLS * CD * SEQS, dtype=jnp.int32) % SEQS)[picked]
    slot_place = positions.reshape(-1)[picked]
    margins = jnp.zeros((SEQS, LEN), jnp.float32).at[seq_ids, slot_place].set(margin_rows.reshape(MASKED))
    return (expected.reshape(SLOT_COLS, CD, SEQS, D), margins)
```

```python
import functools

import jax
import jax.numpy as jnp
from jax import lax
from jax.experimental import pallas as pl
from jax.experimental.pallas import tpu as pltpu
from jax.sharding import PartitionSpec as P

MESH = pl.DeviceIdType.MESH
F32 = jnp.float32
BF16 = jnp.bfloat16

D = 4096
LEN_DEV = 10
NY, NZ, NX, NC = 4, 8, 4, 2
NK = NX * NC
CAPR = 6
ROWS = NK * CAPR
M = NK * ROWS
V = 1280
H = 2
DH = D // H
CW = DH // NK
SLOTS = 10
SP = 16


def onehot(cond):
    return jnp.where(cond, 1.0, 0.0).astype(BF16)


def iota(shape, dim):
    return lax.broadcasted_iota(jnp.int32, shape, dim)


def div48(i):
    return lax.shift_right_logical(i * 683, 15)


def div6(i):
    return lax.shift_right_logical(i * 43, 8)


def merge(parts):
    top = functools.reduce(jnp.maximum, [p[0] for p in parts])
    total = sum(p[2] * jnp.exp(p[0] - top) for p in parts)
    m1, m2 = parts[0][0], parts[0][1]
    for p in parts[1:]:
        m2 = jnp.maximum(jnp.minimum(m1, p[0]), jnp.maximum(m2, p[1]))
        m1 = jnp.maximum(m1, p[0])
    return m1, m2, total


def kernel(
    q_ref, sc_ref, gain_ref, e_hbm, cnt_ref,
    out_ref, marg_ref,
    e_v, xcat, sb, yr, g, perm, x_v, l_v, p_v, tt, fsc, o32, obf, cr, xs, xr, pst, zs, zr, ys, yr2,
    st_c, st_x, st_z, st_o,
    esem, ysend, yrecv, zsend, zrecv, xsend, xrecv, csend, crecv,
    c2send, c2recv, x2send, x2recv, z2send, z2recv, y2send, y2recv,
    scs, scr, sxs, sxr, szs, szr, ms, mr,
):
    y = lax.axis_index("pos")
    v = lax.axis_index("vocab")
    z = v // NK
    k = lax.rem(v, NK)
    x = k // NC
    c = lax.rem(k, NC)

    def dev(yy, zz, xx, cc):
        return (yy, zz * NK + xx * NC + cc)

    def ypart(o):
        return dev(lax.rem(y + o, NY), z, x, c)

    def zpart(o):
        return dev(y, lax.rem(z + o, NZ), x, c)

    def xpart(o):
        return dev(y, z, lax.rem(x + o, NX), c)

    cpart = dev(y, z, x, 1 - c)
    yoffs, zoffs, xoffs = (1, 3, 2), (4, 3, 5, 2, 6, 1, 7), (2, 1, 3)
    pending = []

    def send(src, dst, ss, rs, to):
        cp = pltpu.make_async_remote_copy(
            src_ref=src, dst_ref=dst, send_sem=ss, recv_sem=rs, device_id=to, device_id_type=MESH
        )
        cp.start()
        pending.append(cp)
        return cp

    def blk(kk):
        return pl.ds(pl.multiple_of(kk * ROWS, 16), ROWS)

    barrier = pltpu.get_barrier_semaphore()
    partners = [ypart(o) for o in yoffs] + [zpart(o) for o in zoffs]
    partners += [xpart(o) for o in xoffs] + [cpart]
    for to in partners:
        pl.semaphore_signal(barrier, inc=1, device_id=to, device_id_type=MESH)
    e_copy = pltpu.make_async_copy(e_hbm, e_v, esem)
    e_copy.start()

    q = q_ref[...].astype(F32)
    sc = sc_ref[...]
    deq = [q[:, i * 128:(i + 1) * 128] * sc[:, i:i + 1] for i in range(D // 128)]
    sq = sum(d * d for d in deq)
    inv = lax.rsqrt(jnp.sum(sq, axis=1, keepdims=True) * (1.0 / D) + 1e-6)
    xcat[...] = jnp.zeros_like(xcat)
    for i in range(D // 128):
        h, rest = divmod(i * 128, DH)
        cc, lane = divmod(rest, CW)
        gn = gain_ref[:, i * 128:(i + 1) * 128]
        row = (deq[i] * inv * gn).astype(BF16)
        xcat[h, cc * SP:cc * SP + SLOTS, lane:lane + 128] = row

    before = []
    run = jnp.int32(0)
    for s in range(8):
        before.append(run)
        run = run + lax.shift_right_logical(cnt_ref[s] + 63, 6)
    bars = []
    for r5 in range(5):
        for s2 in range(2):
            seq = y * 2 + s2
            first = jnp.int32(0)
            for s in range(8):
                first = jnp.where(seq == s, before[s], first)
            bars.append(jnp.where(r5 * 64 + v < cnt_ref[seq], first + r5, -1))

    def slot_bar(j):
        bar = jnp.full(j.shape, -1, jnp.int32)
        for i, b in enumerate(bars):
            bar = jnp.where(j == i, b, bar)
        return bar

    shape = (NY * ROWS, NK * SP)
    i0 = iota((NY * ROWS, 1), 0)
    o_i = div48(i0)
    ci = div6(i0 - o_i * ROWS)
    ri = i0 - o_i * ROWS - ci * CAPR
    want = ri * NY + jnp.bitwise_and(y + o_i, NY - 1)
    j0 = iota((1, NK * SP), 1)
    cj = lax.shift_right_logical(j0, 4)
    bar_j = slot_bar(jnp.bitwise_and(j0, SP - 1))
    pick = onehot(
        (jnp.broadcast_to(ci, shape) == jnp.broadcast_to(cj, shape))
        & (jnp.broadcast_to(want, shape) == jnp.broadcast_to(bar_j, shape))
    )
    for h in range(H):
        blocks = jnp.dot(pick, xcat[h], preferred_element_type=F32).astype(BF16)
        for o in range(NY):
            sb[h, o] = blocks[o * ROWS:(o + 1) * ROWS]

    pl.semaphore_wait(barrier, len(partners))

    ycp = {}
    for h in range(H):
        for o in yoffs:
            ycp[h, o] = send(sb.at[h, o], yr.at[h, o], ysend.at[h, o], yrecv.at[h, o], ypart(o))

    pi = iota((M, 1), 0)
    pa = div48(pi)
    pb = div6(pi - pa * ROWS)
    pr = pi - pa * ROWS - pb * CAPR
    perm[...] = onehot(
        jnp.broadcast_to(pb * ROWS + pa * CAPR + pr, (M, M)) == iota((M, M), 1)
    )

    zcp = {}
    for h in range(H):
        for o in yoffs:
            ycp[h, o].wait_recv()
        own = sb[h, 0].astype(F32)
        for o in yoffs:
            own = own + yr[h, o].astype(F32)
        g[h, blk(z), :] = own.astype(BF16)
        for o in zoffs:
            zcp[h, o] = send(
                g.at[h, blk(z)], g.at[h, blk(z)], zsend.at[h, o], zrecv.at[h, o], zpart(o)
            )

    xcp, ccp = {}, {}

    def half(ref, rows, h):
        return ref.at[rows, pl.ds(h * DH, DH)]

    for h in range(H):
        for o in zoffs:
            zcp[h, o].wait_recv()
        lines = jnp.dot(perm[...], g[h], preferred_element_type=F32).astype(BF16)
        for cc in range(NK):
            x_v[blk(k), h * DH + cc * CW:h * DH + (cc + 1) * CW] = lines[cc * ROWS:(cc + 1) * ROWS]
        mine = half(x_v, blk(k), h)
        for o in xoffs:
            xcp[h, o] = send(mine, mine, xsend.at[h, o], xrecv.at[h, o], xpart(o))
        ccp[h, 0] = send(mine, mine, csend.at[h, 0], crecv.at[h, 0], cpart)

    for h in range(H):
        for o in (1, 3, 2):
            xcp[h, o].wait_recv()
            got = half(x_v, blk(lax.rem(x + NX - o, NX) * NC + c), h)
            ccp[h, o] = send(got, got, csend.at[h, o], crecv.at[h, o], cpart)
        for o in (0, 1, 3, 2):
            ccp[h, o].wait_recv()
        if h == 0:
            e_copy.wait()

        def mm1(i, carry):
            n = pl.ds(pl.multiple_of(i * 256, 256), 256)
            part = lax.dot_general(
                x_v[:, h * DH:(h + 1) * DH], e_v[n, h * DH:(h + 1) * DH],
                (((1,), (1,)), ((), ())), preferred_element_type=F32,
            )
            l_v[:, n] = part if h == 0 else l_v[:, n] + part
            return carry

        lax.fori_loop(0, V // 256, mm1, 0)

    def stats(i, carry):
        r = pl.ds(pl.multiple_of(i * 128, 128), 128)
        t1 = l_v[r, 0:128]
        t2 = jnp.full((128, 128), -jnp.inf, F32)
        for j in range(1, V // 128):
            val = l_v[r, j * 128:(j + 1) * 128]
            t2 = jnp.maximum(t2, jnp.minimum(t1, val))
            t1 = jnp.maximum(t1, val)
        top = jnp.max(t1, axis=1, keepdims=True)
        acc = jnp.zeros((128, 128), F32)
        for j in range(V // 128):
            e = jnp.exp(l_v[r, j * 128:(j + 1) * 128] - top)
            acc = acc + e
            p_v[r, j * 128:(j + 1) * 128] = e.astype(BF16)
        tt[0, :, r] = t1.T
        tt[1, :, r] = t2.T
        tt[2, :, r] = acc.T
        return carry

    for i in range(M // 128):
        stats(i, 0)
    m1, m2, sm = tt[0], tt[1], tt[2]
    n = 128
    while n > 1:
        n //= 2
        a1, b1 = m1[:n], m1[n:]
        m2 = jnp.maximum(jnp.minimum(a1, b1), jnp.maximum(m2[:n], m2[n:]))
        m1 = jnp.maximum(a1, b1)
        sm = sm[:n] + sm[n:]
    loc = m1

    def put(slot, parts):
        st_o[slot, 0:1] = parts[0]
        st_o[slot, 1:2] = parts[1]
        st_o[slot, 2:3] = parts[2]

    def got3(ref):
        return (ref[0:1], ref[1:2], ref[2:3])

    def mm2(h, lo, hi):
        def body(i, carry):
            n = pl.ds(pl.multiple_of(h * DH + i * 256, 256), 256)
            o32[:, n] = jnp.dot(p_v[...], e_v[:, n], preferred_element_type=F32)
            return carry

        lax.fori_loop(lo, hi, body, 0)

    half_n = DH // 512
    st_o[...] = jnp.zeros_like(st_o)
    cur = (m1, m2, sm)
    put(0, cur)
    cp = send(st_o.at[0], st_c, scs, scr, cpart)
    mm2(0, 0, half_n)
    cp.wait_recv()
    cur = merge([cur, got3(st_c)])
    put(1, cur)
    cps = [send(st_o.at[1], st_x.at[o], sxs.at[o], sxr.at[o], xpart(o)) for o in xoffs]
    mm2(0, half_n, 2 * half_n)
    for cp in cps:
        cp.wait_recv()
    cur = merge([cur] + [got3(st_x[o]) for o in xoffs])
    put(2, cur)
    cps = [send(st_o.at[2], st_z.at[o], szs.at[o], szr.at[o], zpart(o)) for o in zoffs]
    mm2(1, 0, half_n)
    for cp in cps:
        cp.wait_recv()
    m1, m2, sm = merge([cur] + [got3(st_z[o]) for o in zoffs])
    factor = jnp.exp(loc - m1) / sm * 64.0
    for i in range(M // 128):
        fsc[i * 128:(i + 1) * 128] = jnp.broadcast_to(factor[:, i * 128:(i + 1) * 128], (128, 128)).T
    margin = (1.0 - jnp.exp(m2 - m1)) / sm
    marg_ref[y] = jnp.broadcast_to(margin, (8, M))
    mcp = [send(marg_ref.at[y], marg_ref.at[y], ms.at[o], mr.at[o], ypart(o)) for o in yoffs]

    def scale(h):
        def body(i, carry):
            n = pl.ds(pl.multiple_of(h * DH + i * 128, 128), 128)
            obf[:, n] = (o32[:, n] * fsc[...]).astype(BF16)
            return carry

        lax.fori_loop(0, DH // 128, body, 0)

    c2, x2, z2, y2 = {}, {}, {}, {}

    def core_send(h):
        for o in (2, 1, 3, 0):
            xx = lax.rem(x + o, NX)
            c2[h, o] = send(
                half(obf, blk(xx * NC + 1 - c), h), cr.at[h, o], c2send.at[h, o], c2recv.at[h, o], cpart
            )

    scale(0)
    core_send(0)
    mm2(1, half_n, 2 * half_n)
    scale(1)
    core_send(1)
    for h in range(H):
        for o in (2, 1, 3, 0):
            c2[h, o].wait_recv()
            mine = obf[blk(lax.rem(x + o, NX) * NC + c), h * DH:(h + 1) * DH]
            xs[h, o] = (mine.astype(F32) + cr[h, o].astype(F32)).astype(BF16)
            if o:
                x2[h, o] = send(xs.at[h, o], xr.at[h, o], x2send.at[h, o], x2recv.at[h, o], xpart(o))
    for h in range(H):
        for o in xoffs:
            x2[h, o].wait_recv()
        for cc in range(NK):
            ln = slice(cc * CW, (cc + 1) * CW)
            tot = xs[h, 0, :, ln].astype(F32)
            for o in xoffs:
                tot = tot + xr[h, o, :, ln].astype(F32)
            pst[cc * ROWS:(cc + 1) * ROWS] = tot.astype(BF16)
        zs[h] = jnp.dot(perm[...], pst[...], preferred_element_type=F32).astype(BF16)
        for o in zoffs:
            z2[h, o] = send(
                zs.at[h, blk(lax.rem(z + o, NZ))], zr.at[h, o], z2send.at[h, o], z2recv.at[h, o], zpart(o)
            )
    for h in range(H):
        for o in zoffs:
            z2[h, o].wait_recv()
        tot = zs[h, blk(z), :].astype(F32)
        for o in zoffs:
            tot = tot + zr[h, o].astype(F32)
        ys[h] = tot.astype(BF16)
        yr2[h, 0] = ys[h]
        for o in yoffs:
            y2[h, o] = send(ys.at[h], yr2.at[h, o], y2send.at[h, o], y2recv.at[h, o], ypart(o))

    shape = (NK * SP, NY * ROWS)
    j0 = iota((1, NY * ROWS), 1)
    o_j = div48(j0)
    cj = div6(j0 - o_j * ROWS)
    rj = j0 - o_j * ROWS - cj * CAPR
    have = rj * NY + jnp.bitwise_and(y + NY - o_j, NY - 1)
    i0 = iota((NK * SP, 1), 0)
    ci = lax.shift_right_logical(i0, 4)
    bar_i = slot_bar(jnp.bitwise_and(i0, SP - 1))
    back = onehot(
        (jnp.broadcast_to(ci, shape) == jnp.broadcast_to(cj, shape))
        & (jnp.broadcast_to(bar_i, shape) == jnp.broadcast_to(have, shape))
    )
    for h in range(H):
        for o in yoffs:
            y2[h, o].wait_recv()
        cat = jnp.concatenate([yr2[h, o] for o in range(NY)], axis=0)
        res = jnp.dot(back, cat, preferred_element_type=F32).astype(BF16)
        for cc in range(NK):
            out_ref[:, h * DH + cc * CW:h * DH + (cc + 1) * CW] = res[cc * SP:(cc + 1) * SP]

    for cp in mcp:
        cp.wait_recv()
    for cp in pending:
        cp.wait_send()


def readout(q, sc, gain, table, counts):
    dma = pltpu.SemaphoreType.DMA
    vm = pl.BlockSpec(memory_space=pltpu.VMEM)
    return pl.pallas_call(
        kernel,
        out_shape=(
            jax.ShapeDtypeStruct((SP, D), BF16),
            jax.ShapeDtypeStruct((NY, 8, M), F32),
        ),
        in_specs=[vm, vm, vm, pl.BlockSpec(memory_space=pl.ANY), pl.BlockSpec(memory_space=pltpu.SMEM)],
        out_specs=(vm, vm),
        scratch_shapes=[
            pltpu.VMEM((V, D), BF16),
            pltpu.VMEM((H, NK * SP, CW), BF16),
            pltpu.VMEM((H, NY, ROWS, CW), BF16),
            pltpu.VMEM((H, NY, ROWS, CW), BF16),
            pltpu.VMEM((H, M, CW), BF16),
            pltpu.VMEM((M, M), BF16),
            pltpu.VMEM((M, D), BF16),
            pltpu.VMEM((M, V), F32),
            pltpu.VMEM((M, V), BF16),
            pltpu.VMEM((3, 128, M), F32),
            pltpu.VMEM((M, 128), F32),
            pltpu.VMEM((M, D), F32),
            pltpu.VMEM((M, D), BF16),
            pltpu.VMEM((H, NX, ROWS, DH), BF16),
            pltpu.VMEM((H, NX, ROWS, DH), BF16),
            pltpu.VMEM((H, NX, ROWS, DH), BF16),
            pltpu.VMEM((M, CW), BF16),
            pltpu.VMEM((H, M, CW), BF16),
            pltpu.VMEM((H, NZ, ROWS, CW), BF16),
            pltpu.VMEM((H, ROWS, CW), BF16),
            pltpu.VMEM((H, NY, ROWS, CW), BF16),
            pltpu.VMEM((8, M), F32),
            pltpu.VMEM((NX, 8, M), F32),
            pltpu.VMEM((NZ, 8, M), F32),
            pltpu.VMEM((3, 8, M), F32),
            dma,
            dma((H, NY)), dma((H, NY)), dma((H, NZ)), dma((H, NZ)),
            dma((H, NX)), dma((H, NX)), dma((H, NX)), dma((H, NX)),
            dma((H, NX)), dma((H, NX)), dma((H, NX)), dma((H, NX)),
            dma((H, NZ)), dma((H, NZ)), dma((H, NY)), dma((H, NY)),
            dma, dma, dma((NX,)), dma((NX,)), dma((NZ,)), dma((NZ,)), dma((NY,)), dma((NY,)),
        ],
        compiler_params=pltpu.CompilerParams(
            collective_id=0, has_side_effects=True, vmem_limit_bytes=60 << 20
        ),
        cost_estimate=pl.CostEstimate(
            flops=4 * M * V * D, bytes_accessed=2 * V * D, transcendentals=M * V
        ),
        name="readout",
    )(q, sc, gain, table, counts)


def on_device(quantized, scales, norm_gain, embed_table, counts, positions):
    col = lax.axis_index("vocab")
    grp = lax.axis_index("pos")
    rows, seqs = quantized.shape[1], quantized.shape[2]
    out, marg = readout(
        quantized.reshape(SLOTS, D), scales.reshape(SLOTS, D // 128), norm_gain.reshape(1, D),
        embed_table, counts,
    )
    expected = out[:SLOTS].reshape(1, rows, seqs, D)
    by_bar = marg[:, 0].reshape(NY, NK, NZ, CAPR).transpose(3, 0, 2, 1).reshape(NY * CAPR, NZ * NK)
    filled = (counts + 63) // 64
    first = jnp.cumsum(filled) - filled
    own_first = lax.dynamic_slice_in_dim(first, grp * seqs, seqs)
    own_counts = lax.dynamic_slice_in_dim(counts, grp * seqs, seqs)
    row = jnp.arange(rows, dtype=jnp.int32)[:, None]
    bar = jnp.minimum(own_first[None] + row, NY * CAPR - 1)
    values = by_bar[bar]
    slot = row[..., None] * (NZ * NK) + jnp.arange(NZ * NK, dtype=jnp.int32)
    values = jnp.where(slot < own_counts[None, :, None], values, 0.0)
    targets = col * LEN_DEV + jnp.arange(LEN_DEV, dtype=jnp.int32)
    hits = positions.transpose(1, 2, 0)[..., None] == targets
    margins = jnp.sum(jnp.where(hits, values[..., None], 0.0), axis=(0, 2))
    return (expected, margins)


def solution(mesh):
    in_specs = (
        P("vocab", None, "pos", None),
        P("vocab", None, "pos", None),
        P(),
        P("vocab", None),
        P(),
        P(None, None, "pos"),
    )
    out_specs = (P("vocab", None, "pos", None), P("pos", "vocab"))
    return jax.shard_map(
        on_device, mesh=mesh, in_specs=in_specs, out_specs=out_specs, check_vma=False
    )
```

```python
import functools

import jax
import jax.numpy as jnp
from jax import lax
from jax.experimental import pallas as pl
from jax.experimental.pallas import tpu as pltpu
from jax.sharding import PartitionSpec as P

MESH = pl.DeviceIdType.MESH
F32 = jnp.float32
BF16 = jnp.bfloat16

D = 4096
LEN_DEV = 10
NY, NZ, NX, NC = 4, 8, 4, 2
NK = NX * NC
CAPR = 6
ROWS = NK * CAPR
GR = NZ * ROWS
LR = 32
OVR = 2
MAIN = NK * LR
OV = NK * OVR
M = MAIN + OV
ML = 384
V = 1280
H = 2
DH = D // H
CW = DH // NK
SLOTS = 10
SP = 16
BARS = 40


def onehot(cond):
    return jnp.where(cond, 1.0, 0.0).astype(BF16)


def iota(shape, dim):
    return lax.broadcasted_iota(jnp.int32, shape, dim)


def div48(i):
    return lax.shift_right_logical(i * 683, 15)


def div6(i):
    return lax.shift_right_logical(i * 43, 8)


def count(cond, axis):
    return jnp.sum(jnp.where(cond, 1.0, 0.0), axis=axis, keepdims=True).astype(jnp.int32)


def merge(parts):
    top = functools.reduce(jnp.maximum, [p[0] for p in parts])
    total = sum(p[2] * jnp.exp(p[0] - top) for p in parts)
    m1, m2 = parts[0][0], parts[0][1]
    for p in parts[1:]:
        m2 = jnp.maximum(jnp.minimum(m1, p[0]), jnp.maximum(m2, p[1]))
        m1 = jnp.maximum(m1, p[0])
    return m1, m2, total


def kernel(
    q_ref, sc_ref, gain_ref, e_hbm, cnt_ref, pos_ref,
    out_ref, marg_ref,
    e_v, qf, sf, xcat, sb, yr, g, perm1, perm2, swap, back, x_v, ov_g, l_v, p_v, tt, fsc, fs2, o32, obf,
    ovo, cr, cro, xs, xr, pst, zs, zr, ys, yr2, res, mg, st_c, st_x, st_z, st_o,
    esem, ysend, yrecv, zsend, zrecv, xsend, xrecv, csend, crecv,
    vsend, vrecv, wsend, wrecv,
    c2send, c2recv, x2send, x2recv, z2send, z2recv, y2send, y2recv,
    scs, scr, sxs, sxr, szs, szr, ms, mr,
):
    y = lax.axis_index("pos")
    v = lax.axis_index("vocab")
    z = v // NK
    k = lax.rem(v, NK)
    x = k // NC
    c = lax.rem(k, NC)
    line = c * NX + x

    def dev(yy, zz, xx, cc):
        return (yy, zz * NK + xx * NC + cc)

    def xo(o):
        return lax.rem(x + o, NX)

    def ypart(o):
        return dev(lax.rem(y + o, NY), z, x, c)

    def zpart(o):
        return dev(y, lax.rem(z + o, NZ), x, c)

    def xpart(o):
        return dev(y, z, xo(o), c)

    cpart = dev(y, z, x, 1 - c)
    yoffs, zoffs, xoffs = (1, 3, 2), (4, 3, 5, 2, 6, 1, 7), (2, 1, 3)
    pending = []

    def send(src, dst, ss, rs, to):
        cp = pltpu.make_async_remote_copy(
            src_ref=src, dst_ref=dst, send_sem=ss, recv_sem=rs, device_id=to, device_id_type=MESH
        )
        cp.start()
        pending.append(cp)
        return cp

    def rows(start, size):
        return pl.ds(pl.multiple_of(start, 16), size)

    def cols(h):
        return slice(h * DH, (h + 1) * DH)

    barrier = pltpu.get_barrier_semaphore()
    partners = [ypart(o) for o in yoffs] + [zpart(o) for o in zoffs]
    partners += [xpart(o) for o in xoffs] + [cpart]
    for to in partners:
        pl.semaphore_signal(barrier, inc=1, device_id=to, device_id_type=MESH)
    e_copy = pltpu.make_async_copy(e_hbm, e_v, esem)
    e_copy.start()

    for i in range(5):
        qf[2 * i:2 * i + 2] = q_ref[i].astype(F32)
        sf[2 * i:2 * i + 2] = sc_ref[i]
    deq = [qf[:SLOTS, i * 128:(i + 1) * 128] * sf[:SLOTS, i:i + 1] for i in range(D // 128)]
    sq = sum(d * d for d in deq)
    inv = lax.rsqrt(jnp.sum(sq, axis=1, keepdims=True) * (1.0 / D) + 1e-6)
    xcat[...] = jnp.zeros_like(xcat)
    for i in range(D // 128):
        h, rest = divmod(i * 128, DH)
        cc, lane = divmod(rest, CW)
        gn = gain_ref[:, i * 128:(i + 1) * 128]
        xcat[h, cc * SP:cc * SP + SLOTS, lane:lane + 128] = (deq[i] * inv * gn).astype(BF16)

    def bar_len(seq, row):
        n = jnp.zeros(seq.shape, jnp.int32)
        for s in range(8):
            n = jnp.where(seq == s, cnt_ref[s], n)
        return jnp.clip(n - 64 * row, 0, 64)

    def bar_axis(dim):
        b = iota((1, 128) if dim == 1 else (BARS, 1), dim)
        return b, jnp.where(b < BARS, bar_len(jnp.bitwise_and(b, 7), lax.shift_right_logical(b, 3)), 0)

    def rank_of(seq, row, dim):
        b, lb = bar_axis(dim)
        mine, ml = row * 8 + seq, bar_len(seq, row)
        return count((lb > ml) | ((lb == ml) & (b < mine)), dim), ml

    def depth(kk, dim):
        _, lb = bar_axis(dim)
        return lax.shift_right_logical(jnp.maximum(lb - kk, 0) + 7, 3)

    def ahead(zz, nz, dim):
        return jnp.sum(jnp.minimum(zz, nz).astype(F32), axis=dim, keepdims=True).astype(jnp.int32)

    def slot_code(i, dim):
        seq, row = y * 2 + jnp.bitwise_and(i, 1), lax.shift_right_logical(i, 1)
        rank, ml = rank_of(seq, row, dim)
        before = ahead(jnp.full(i.shape, z, jnp.int32), depth(k, dim), dim)
        code = jnp.bitwise_and(rank + before, 3) * 8 + lax.shift_right_logical(rank, 2)
        return jnp.where((v < ml) & (i < SLOTS), code, -1)

    shape = (NY * ROWS, NK * SP)
    i0 = iota((NY * ROWS, 1), 0)
    o_i = div48(i0)
    ci = div6(i0 - o_i * ROWS)
    ri = i0 - o_i * ROWS - ci * CAPR
    want = jnp.bitwise_and(y + o_i, NY - 1) * 8 + ri
    j0 = iota((1, NK * SP), 1)
    cj = lax.shift_right_logical(j0, 4)
    code_j = slot_code(jnp.bitwise_and(j0, SP - 1), 0)
    pick = onehot(
        (jnp.broadcast_to(ci, shape) == jnp.broadcast_to(cj, shape))
        & (jnp.broadcast_to(want, shape) == jnp.broadcast_to(code_j, shape))
    )
    for h in range(H):
        blocks = jnp.dot(pick, xcat[h], preferred_element_type=F32).astype(BF16)
        for o in range(NY):
            sb[h, o] = blocks[o * ROWS:(o + 1) * ROWS]

    pl.semaphore_wait(barrier, len(partners))

    ycp = {}
    for h in range(H):
        for o in yoffs:
            ycp[h, o] = send(sb.at[h, o], yr.at[h, o], ysend.at[h, o], yrecv.at[h, o], ypart(o))

    def place(i, dim):
        zz = div48(i)
        cc = div6(i - zz * ROWS)
        rr = i - zz * ROWS - cc * CAPR
        nz = depth(k, dim)
        before = ahead(zz, nz, dim)
        live = count(nz > zz, dim)
        rank = 4 * rr + jnp.bitwise_and(y - before, 3)
        p = lax.shift_right_logical(before + rank, 2)
        at = jnp.where(p < LR, cc * LR + p, MAIN + cc * OVR + p - LR)
        return jnp.where(rank < live, at, -1)

    perm1[...] = onehot(jnp.broadcast_to(place(iota((1, GR), 1), 0), (M, GR)) == iota((M, GR), 0))

    zcp = {}
    for h in range(H):
        for o in yoffs:
            ycp[h, o].wait_recv()
        own = sb[h, 0].astype(F32)
        for o in yoffs:
            own = own + yr[h, o].astype(F32)
        g[h, rows(z * ROWS, ROWS), :] = own.astype(BF16)
        for o in zoffs:
            mine = g.at[h, rows(z * ROWS, ROWS)]
            zcp[h, o] = send(mine, mine, zsend.at[h, o], zrecv.at[h, o], zpart(o))

    si = iota((128, 1), 0)
    sa, sbb = lax.shift_right_logical(si, 4), jnp.bitwise_and(lax.shift_right_logical(si, 1), 7)
    swap[...] = onehot(
        jnp.broadcast_to(sbb * 16 + sa * 2 + jnp.bitwise_and(si, 1), (128, 128)) == iota((128, 128), 1)
    )
    perm2[...] = onehot(
        jnp.broadcast_to(place(iota((GR, 1), 0), 1), (GR, M)) == iota((GR, M), 1)
    )
    shape = (NK * SP, NY * ROWS)
    j0 = iota((1, NY * ROWS), 1)
    o_j = div48(j0)
    cj = div6(j0 - o_j * ROWS)
    rj = j0 - o_j * ROWS - cj * CAPR
    have = jnp.bitwise_and(y + NY - o_j, NY - 1) * 8 + rj
    i0 = iota((NK * SP, 1), 0)
    ci = lax.shift_right_logical(i0, 4)
    code_i = slot_code(jnp.bitwise_and(i0, SP - 1), 1)
    back[...] = onehot(
        (jnp.broadcast_to(ci, shape) == jnp.broadcast_to(cj, shape))
        & (jnp.broadcast_to(code_i, shape) == jnp.broadcast_to(have, shape))
    )

    xcp, ccp, vcp, wcp = {}, {}, {}, {}

    def main_at(ln, h):
        return x_v.at[rows(ln * LR, LR), pl.ds(h * DH, DH)]

    def further_at(ln, h):
        return ov_g.at[h, rows(ln * OV, OV)]

    def x_send(ln, h, o, to):
        a, b = main_at(ln, h), further_at(ln, h)
        xcp[h, o] = send(a, a, xsend.at[h, o], xrecv.at[h, o], to)
        vcp[h, o] = send(b, b, vsend.at[h, o], vrecv.at[h, o], to)

    def c_send(ln, h, o):
        a, b = main_at(ln, h), further_at(ln, h)
        ccp[h, o] = send(a, a, csend.at[h, o], crecv.at[h, o], cpart)
        wcp[h, o] = send(b, b, wsend.at[h, o], wrecv.at[h, o], cpart)

    for h in range(H):
        for o in zoffs:
            zcp[h, o].wait_recv()
        lines = jnp.dot(perm1[...], g[h], preferred_element_type=F32).astype(BF16)
        for cc in range(NK):
            ln = slice(h * DH + cc * CW, h * DH + (cc + 1) * CW)
            x_v[rows(line * LR, LR), ln] = lines[cc * LR:(cc + 1) * LR]
        ov_g[h, rows(line * OV, OV)] = lines[MAIN:]
        x_send(line, h, 1, xpart(1))
        x_send(line, h, 3, xpart(3))
        c_send(line, h, 0)

    def x_got(h, o):
        xcp[h, o].wait_recv()
        vcp[h, o].wait_recv()

    for h, o in ((0, 1), (1, 3)):
        x_got(h, o)
        ln = c * NX + xo(NX - o)
        x_send(ln, h, 2, xpart(o))
        c_send(ln, h, o)
        other = NX - o
        x_got(h, other)
        c_send(c * NX + xo(NX - other), h, other)

    for h in range(H):
        x_got(h, 2)
        c_send(c * NX + xo(2), h, 2)
        for o in (0, 1, 3, 2):
            ccp[h, o].wait_recv()
            wcp[h, o].wait_recv()
        further = jnp.dot(swap[...], ov_g[h], preferred_element_type=F32).astype(BF16)
        for cc in range(NK):
            x_v[MAIN:, h * DH + cc * CW:h * DH + (cc + 1) * CW] = further[cc * OV:(cc + 1) * OV]
        if h == 0:
            e_copy.wait()

        def mm1(i, carry):
            n = pl.ds(pl.multiple_of(i * 256, 256), 256)
            part = lax.dot_general(
                x_v[:, cols(h)], e_v[n, cols(h)],
                (((1,), (1,)), ((), ())), preferred_element_type=F32,
            )
            l_v[:, n] = part if h == 0 else l_v[:, n] + part
            return carry

        lax.fori_loop(0, V // 256, mm1, 0)

    for start, size in ((0, 128), (128, 128), (MAIN, OV)):
        r = slice(start, start + size)
        t1 = l_v[r, 0:128]
        t2 = jnp.full((size, 128), -jnp.inf, F32)
        for j in range(1, V // 128):
            val = l_v[r, j * 128:(j + 1) * 128]
            t2 = jnp.maximum(t2, jnp.minimum(t1, val))
            t1 = jnp.maximum(t1, val)
        top = jnp.max(t1, axis=1, keepdims=True)
        acc = jnp.zeros((size, 128), F32)
        for j in range(V // 128):
            e = jnp.exp(l_v[r, j * 128:(j + 1) * 128] - top)
            acc = acc + e
            p_v[r, j * 128:(j + 1) * 128] = e.astype(BF16)
        if size < 128:
            pad = jnp.ones((128 - size, 128), F32)
            t1, t2, acc = (jnp.concatenate([a, pad], axis=0) for a in (t1, t2, acc))
        for n, a in enumerate((t1, t2, acc)):
            tt[n, :, start:start + 128] = a.T
    m1, m2, sm = tt[0], tt[1], tt[2]
    n = 128
    while n > 1:
        n //= 2
        a1, b1 = m1[:n], m1[n:]
        m2 = jnp.maximum(jnp.minimum(a1, b1), jnp.maximum(m2[:n], m2[n:]))
        m1 = jnp.maximum(a1, b1)
        sm = sm[:n] + sm[n:]
    loc = m1

    def put(slot, parts):
        for n in range(3):
            st_o[slot, n:n + 1] = parts[n]

    def got3(ref):
        return (ref[0:1], ref[1:2], ref[2:3])

    def spread(ref, factor):
        for i in range(0, ML, 128):
            size = min(128, M - i)
            ref[i:i + size] = jnp.broadcast_to(factor[:, i:i + 128], (128, 128)).T[:size]

    def mm2(lo, hi):
        def body(i, carry):
            n = pl.ds(pl.multiple_of(i * 256, 256), 256)
            o32[:, n] = jnp.dot(p_v[...], e_v[:, n], preferred_element_type=F32)
            return carry

        lax.fori_loop(lo, hi, body, 0)

    quarter = DH // 512
    st_o[...] = jnp.zeros_like(st_o)
    cur = (m1, m2, sm)
    put(0, cur)
    cp = send(st_o.at[0], st_c, scs, scr, cpart)
    mm2(0, quarter)
    cp.wait_recv()
    cur = merge([cur, got3(st_c)])
    put(1, cur)
    cps = [send(st_o.at[1], st_x.at[o], sxs.at[o], sxr.at[o], xpart(o)) for o in xoffs]
    mm2(quarter, 2 * quarter)
    for cp in cps:
        cp.wait_recv()
    cur = merge([cur] + [got3(st_x[o]) for o in xoffs])
    put(2, cur)
    scp = [send(st_o.at[2], st_z.at[o], szs.at[o], szr.at[o], zpart(o)) for o in zoffs]
    spread(fsc, jnp.exp(loc - cur[0]))

    c2, x2, z2, y2 = {}, {}, {}, {}

    def scaled(i, carry):
        n = pl.ds(pl.multiple_of(i * 128, 128), 128)
        obf[:, n] = (o32[:, n] * fsc[...]).astype(BF16)
        return carry

    def mm2_scaled(i, carry):
        n = pl.ds(pl.multiple_of(i * 256, 256), 256)
        part = jnp.dot(p_v[...], e_v[:, n], preferred_element_type=F32)
        for t in range(2):
            at = pl.ds(pl.multiple_of(i * 256 + t * 128, 128), 128)
            obf[:, at] = (part[:, t * 128:(t + 1) * 128] * fsc[...]).astype(BF16)
        return carry

    def core_send(h):
        src = obf.at[rows((1 - c) * NX * LR, NX * LR), pl.ds(h * DH, DH)]
        c2[h, 0] = send(src, cr.at[h], c2send.at[h, 0], c2recv.at[h, 0], cpart)
        stack = jnp.concatenate(
            [obf[MAIN:, h * DH + cc * CW:h * DH + (cc + 1) * CW] for cc in range(NK)], axis=0
        )
        ovo[h] = jnp.dot(swap[...], stack, preferred_element_type=F32).astype(BF16)
        src = ovo.at[h, rows((1 - c) * NX * OV, NX * OV)]
        c2[h, 1] = send(src, cro.at[h], c2send.at[h, 1], c2recv.at[h, 1], cpart)

    lax.fori_loop(0, DH // 128, scaled, 0)
    core_send(0)
    lax.fori_loop(DH // 256, D // 256, mm2_scaled, 0)
    core_send(1)

    def x2_send(h, o, to):
        x2[h, o] = send(xs.at[h, o], xr.at[h, o], x2send.at[h, o], x2recv.at[h, o], xpart(to))

    def chip_sum(h, o):
        xx = xo(o)
        at = rows((c * NX + xx) * LR, LR)
        for cc in range(NK):
            mine = obf[at, h * DH + cc * CW:h * DH + (cc + 1) * CW].astype(F32)
            theirs = cr[h, rows(xx * LR, LR), cc * CW:(cc + 1) * CW].astype(F32)
            xs[h, o, cc * LR:(cc + 1) * LR] = (mine + theirs).astype(BF16)
        mine = ovo[h, rows((c * NX + xx) * OV, OV)].astype(F32)
        theirs = cro[h, rows(xx * OV, OV)].astype(F32)
        xs[h, o, MAIN:] = (mine + theirs).astype(BF16)

    for h, o in ((0, 1), (1, 3)):
        c2[h, 0].wait_recv()
        c2[h, 1].wait_recv()
        chip_sum(h, 2)
        x2_send(h, 2, o)
        chip_sum(h, NX - o)
        x2_send(h, NX - o, NX - o)
        chip_sum(h, o)
        chip_sum(h, 0)
    for h, o in ((0, 1), (1, 3)):
        x2[h, 2].wait_recv()
        xs[h, o] = (xs[h, o].astype(F32) + xr[h, 2].astype(F32)).astype(BF16)
        x2_send(h, o, o)

    for cp in scp:
        cp.wait_recv()
    m8 = cur[0]
    m1, m2, sm = merge([cur] + [got3(st_z[o]) for o in zoffs])
    spread(fs2, jnp.exp(m8 - m1) / sm * 64.0)
    margin = (1.0 - jnp.exp(m2 - m1)) / sm
    mg[y] = jnp.broadcast_to(margin, (8, ML))
    mcp = [send(mg.at[y], mg.at[y], ms.at[o], mr.at[o], ypart(o)) for o in yoffs]

    f_main = fs2[rows(line * LR, LR)]
    f_a = fs2[pl.ds(MAIN + line * OVR, 1)]
    f_b = fs2[pl.ds(MAIN + line * OVR + 1, 1)]
    f_ov = jnp.where(jnp.bitwise_and(iota((OV, 128), 0), 1) == 0, f_a, f_b)

    for h in range(H):
        for o in (1, 3):
            x2[h, o].wait_recv()
        for lane in range(0, CW, 128):
            ln = slice(lane, lane + 128)
            for cc in range(NK + 1):
                r = slice(cc * LR, min(cc * LR + LR, M))
                tot = xs[h, 0, r, ln].astype(F32) + xr[h, 1, r, ln].astype(F32)
                tot = tot + xr[h, 3, r, ln].astype(F32)
                pst[r, ln] = (tot * (f_main if cc < NK else f_ov)).astype(BF16)
        zs[h] = jnp.dot(perm2[...], pst[...], preferred_element_type=F32).astype(BF16)
        for o in zoffs:
            src = zs.at[h, rows(lax.rem(z + o, NZ) * ROWS, ROWS)]
            z2[h, o] = send(src, zr.at[h, o], z2send.at[h, o], z2recv.at[h, o], zpart(o))

    for cp in mcp:
        cp.wait_recv()
    lane = iota((1, ML), 1)
    lm = jnp.minimum(lane, M - 1)
    ln = jnp.where(lm < MAIN, lax.shift_right_logical(lm, 5), lax.shift_right_logical(lm - MAIN, 1))
    p = jnp.where(lm < MAIN, jnp.bitwise_and(lm, LR - 1), LR + jnp.bitwise_and(lm, 1))
    kk = jnp.bitwise_and(ln, NX - 1) * NC + lax.shift_right_logical(ln, 2)
    nz = depth(kk, 0)
    befores = [ahead(jnp.full((1, ML), n, jnp.int32), nz, 0) for n in range(NZ + 1)]
    slot = iota((SP, 1), 0)
    rank_i, len_i = rank_of(y * 2 + jnp.bitwise_and(slot, 1), lax.shift_right_logical(slot, 1), 1)
    by_col = jnp.zeros((SP, 64), F32)
    for yy in range(NY):
        gi = 4 * p + yy
        zz = jnp.zeros((1, ML), jnp.int32)
        first = jnp.zeros((1, ML), jnp.int32)
        for n in range(1, NZ):
            past = befores[n] <= gi
            zz = jnp.where(past, n, zz)
            first = jnp.where(past, befores[n], first)
        rank = jnp.where((gi < befores[NZ]) & (lane < M), gi - first, -1)
        vals = jnp.where(
            jnp.broadcast_to(rank, (SP, ML)) == jnp.broadcast_to(rank_i, (SP, ML)),
            jnp.broadcast_to(mg[yy, 0:1], (SP, ML)), 0.0,
        )
        hit = jnp.broadcast_to(zz * NK + kk, (64, ML)) == iota((64, ML), 0)
        by_col = by_col + lax.dot_general(
            vals, jnp.where(hit, 1.0, 0.0), (((1,), (1,)), ((), ())),
            preferred_element_type=F32, precision=lax.Precision.HIGHEST,
        )
    masked = (iota((SP, 64), 1) < len_i) & (iota((SP, 64), 0) < SLOTS)
    by_col = jnp.where(masked, by_col, 0.0)
    wide = (2, 128)
    marg = jnp.zeros(wide, F32)
    for t in range(LEN_DEV):
        target = v * LEN_DEV + t
        for s2 in range(2):
            hit = sum(
                jnp.where(pos_ref[r5, s2:s2 + 1] == target, by_col[2 * r5 + s2:2 * r5 + s2 + 1], 0.0)
                for r5 in range(5)
            )
            val = jnp.broadcast_to(jnp.sum(hit, axis=1, keepdims=True), wide)
            marg = jnp.where((iota(wide, 1) == t) & (iota(wide, 0) == s2), val, marg)
    marg_ref[...] = marg[:, :LEN_DEV]

    for h in range(H):
        for o in zoffs:
            z2[h, o].wait_recv()
        tot = zs[h, rows(z * ROWS, ROWS), :].astype(F32)
        for o in zoffs:
            tot = tot + zr[h, o].astype(F32)
        ys[h] = tot.astype(BF16)
        yr2[h, 0] = ys[h]
        for o in yoffs:
            y2[h, o] = send(ys.at[h], yr2.at[h, o], y2send.at[h, o], y2recv.at[h, o], ypart(o))

    for h in range(H):
        for o in yoffs:
            y2[h, o].wait_recv()
        cat = jnp.concatenate([yr2[h, o] for o in range(NY)], axis=0)
        got = jnp.dot(back[...], cat, preferred_element_type=F32)
        for cc in range(NK):
            res[:, h * DH + cc * CW:h * DH + (cc + 1) * CW] = got[cc * SP:(cc + 1) * SP]
    for i in range(5):
        out_ref[i] = res[2 * i:2 * i + 2].astype(BF16)
    for cp in pending:
        cp.wait_send()


def readout(q, sc, gain, table, counts, positions):
    dma = pltpu.SemaphoreType.DMA
    vm = pl.BlockSpec(memory_space=pltpu.VMEM)
    return pl.pallas_call(
        kernel,
        out_shape=(
            jax.ShapeDtypeStruct(q.shape, BF16),
            jax.ShapeDtypeStruct((2, LEN_DEV), F32),
        ),
        in_specs=[
            vm, vm, vm, pl.BlockSpec(memory_space=pl.ANY), pl.BlockSpec(memory_space=pltpu.SMEM), vm
        ],
        out_specs=(vm, vm),
        scratch_shapes=[
            pltpu.VMEM((V, D), BF16),
            pltpu.VMEM((SP, D), F32),
            pltpu.VMEM((SP, D // 128), F32),
            pltpu.VMEM((H, NK * SP, CW), BF16),
            pltpu.VMEM((H, NY, ROWS, CW), BF16),
            pltpu.VMEM((H, NY, ROWS, CW), BF16),
            pltpu.VMEM((H, GR, CW), BF16),
            pltpu.VMEM((M, GR), BF16),
            pltpu.VMEM((GR, M), BF16),
            pltpu.VMEM((128, 128), BF16),
            pltpu.VMEM((NK * SP, NY * ROWS), BF16),
            pltpu.VMEM((M, D), BF16),
            pltpu.VMEM((H, NK * OV, CW), BF16),
            pltpu.VMEM((M, V), F32),
            pltpu.VMEM((M, V), BF16),
            pltpu.VMEM((3, 128, ML), F32),
            pltpu.VMEM((M, 128), F32),
            pltpu.VMEM((M, 128), F32),
            pltpu.VMEM((M, DH), F32),
            pltpu.VMEM((M, D), BF16),
            pltpu.VMEM((H, NK * OV, CW), BF16),
            pltpu.VMEM((H, NX * LR, DH), BF16),
            pltpu.VMEM((H, NX * OV, CW), BF16),
            pltpu.VMEM((H, NX, M, CW), BF16),
            pltpu.VMEM((H, NX, M, CW), BF16),
            pltpu.VMEM((M, CW), BF16),
            pltpu.VMEM((H, GR, CW), BF16),
            pltpu.VMEM((H, NZ, ROWS, CW), BF16),
            pltpu.VMEM((H, ROWS, CW), BF16),
            pltpu.VMEM((H, NY, ROWS, CW), BF16),
            pltpu.VMEM((SP, D), F32),
            pltpu.VMEM((NY, 8, ML), F32),
            pltpu.VMEM((8, ML), F32),
            pltpu.VMEM((NX, 8, ML), F32),
            pltpu.VMEM((NZ, 8, ML), F32),
            pltpu.VMEM((3, 8, ML), F32),
            dma,
            dma((H, NY)), dma((H, NY)), dma((H, NZ)), dma((H, NZ)),
            dma((H, NX)), dma((H, NX)), dma((H, NX)), dma((H, NX)),
            dma((H, NX)), dma((H, NX)), dma((H, NX)), dma((H, NX)),
            dma((H, 2)), dma((H, 2)), dma((H, NX)), dma((H, NX)),
            dma((H, NZ)), dma((H, NZ)), dma((H, NY)), dma((H, NY)),
            dma, dma, dma((NX,)), dma((NX,)), dma((NZ,)), dma((NZ,)), dma((NY,)), dma((NY,)),
        ],
        compiler_params=pltpu.CompilerParams(
            collective_id=0, has_side_effects=True, vmem_limit_bytes=60 << 20
        ),
        cost_estimate=pl.CostEstimate(
            flops=4 * M * V * D, bytes_accessed=2 * V * D, transcendentals=M * V
        ),
        name="readout",
    )(q, sc, gain, table, counts, positions)


def on_device(quantized, scales, norm_gain, embed_table, counts, positions):
    expected, margins = readout(
        quantized[0], scales[0], norm_gain.reshape(1, D), embed_table, counts,
        positions.transpose(1, 2, 0),
    )
    return (expected[None], margins)


def solution(mesh):
    in_specs = (
        P("vocab", None, "pos", None),
        P("vocab", None, "pos", None),
        P(),
        P("vocab", None),
        P(),
        P(None, None, "pos"),
    )
    out_specs = (P("vocab", None, "pos", None), P("pos", "vocab"))
    return jax.shard_map(
        on_device, mesh=mesh, in_specs=in_specs, out_specs=out_specs, check_vma=False
    )
```

```python
import functools

import jax
import jax.numpy as jnp
from jax import lax
from jax.experimental import pallas as pl
from jax.experimental.pallas import tpu as pltpu
from jax.sharding import PartitionSpec as P

MESH = pl.DeviceIdType.MESH
F32 = jnp.float32
BF16 = jnp.bfloat16

D = 4096
LEN_DEV = 10
NY, NZ, NX, NC = 4, 8, 4, 2
NK = NX * NC
CAPR = 6
ROWS = NK * CAPR
GR = NZ * ROWS
LR = 32
OVR = 2
MAIN = NK * LR
OV = NK * OVR
M = MAIN + OV
ML = 384
V = 1280
H = 2
DH = D // H
CW = DH // NK
SLOTS = 10
SP = 16
BARS = 40


def onehot(cond):
    return jnp.where(cond, 1.0, 0.0).astype(BF16)


def iota(shape, dim):
    return lax.broadcasted_iota(jnp.int32, shape, dim)


def div48(i):
    return lax.shift_right_logical(i * 683, 15)


def div6(i):
    return lax.shift_right_logical(i * 43, 8)


def count(cond, axis):
    return jnp.sum(jnp.where(cond, 1.0, 0.0), axis=axis, keepdims=True).astype(jnp.int32)


def merge(parts):
    top = functools.reduce(jnp.maximum, [p[0] for p in parts])
    total = sum(p[2] * jnp.exp(p[0] - top) for p in parts)
    m1, m2 = parts[0][0], parts[0][1]
    for p in parts[1:]:
        m2 = jnp.maximum(jnp.minimum(m1, p[0]), jnp.maximum(m2, p[1]))
        m1 = jnp.maximum(m1, p[0])
    return m1, m2, total


def kernel(
    q_ref, sc_ref, gain_ref, e_hbm, cnt_ref, pos_ref,
    out_ref, marg_ref,
    e_v, qf, sf, xcat, sb, yr, g, perm1, perm2, swap, back, x_v, ov_g, l_v, p_v, tt, fsc, fs2, obf,
    ovo, cr, cro, xs, xr, pst, zs, zr, ys, yr2, res, mg, st_c, st_x, st_z, st_o,
    esem, ysend, yrecv, zsend, zrecv, xsend, xrecv, csend, crecv,
    vsend, vrecv, wsend, wrecv,
    c2send, c2recv, x2send, x2recv, z2send, z2recv, y2send, y2recv,
    scs, scr, sxs, sxr, szs, szr, ms, mr,
):
    y = lax.axis_index("pos")
    v = lax.axis_index("vocab")
    z = v // NK
    k = lax.rem(v, NK)
    x = k // NC
    c = lax.rem(k, NC)
    line = c * NX + x

    def dev(yy, zz, xx, cc):
        return (yy, zz * NK + xx * NC + cc)

    def xo(o):
        return lax.rem(x + o, NX)

    def ypart(o):
        return dev(lax.rem(y + o, NY), z, x, c)

    def zpart(o):
        return dev(y, lax.rem(z + o, NZ), x, c)

    def xpart(o):
        return dev(y, z, xo(o), c)

    cpart = dev(y, z, x, 1 - c)
    yoffs, zoffs, xoffs = (1, 3, 2), (4, 3, 5, 2, 6, 1, 7), (2, 1, 3)
    pending = []

    def send(src, dst, ss, rs, to):
        cp = pltpu.make_async_remote_copy(
            src_ref=src, dst_ref=dst, send_sem=ss, recv_sem=rs, device_id=to, device_id_type=MESH
        )
        cp.start()
        pending.append(cp)
        return cp

    def rows(start, size):
        return pl.ds(pl.multiple_of(start, 16), size)

    def cols(h):
        return slice(h * DH, (h + 1) * DH)

    barrier = pltpu.get_barrier_semaphore()
    partners = [ypart(o) for o in yoffs] + [zpart(o) for o in zoffs]
    partners += [xpart(o) for o in xoffs] + [cpart]
    for to in partners:
        pl.semaphore_signal(barrier, inc=1, device_id=to, device_id_type=MESH)
    e_copy = pltpu.make_async_copy(e_hbm, e_v, esem)
    e_copy.start()

    for i in range(5):
        qf[2 * i:2 * i + 2] = q_ref[i].astype(F32)
        sf[2 * i:2 * i + 2] = sc_ref[i]
    deq = [qf[:SLOTS, i * 128:(i + 1) * 128] * sf[:SLOTS, i:i + 1] for i in range(D // 128)]
    sq = sum(d * d for d in deq)
    inv = lax.rsqrt(jnp.sum(sq, axis=1, keepdims=True) * (1.0 / D) + 1e-6)
    xcat[...] = jnp.zeros_like(xcat)
    for i in range(D // 128):
        h, rest = divmod(i * 128, DH)
        cc, lane = divmod(rest, CW)
        gn = gain_ref[:, i * 128:(i + 1) * 128]
        xcat[h, cc * SP:cc * SP + SLOTS, lane:lane + 128] = (deq[i] * inv * gn).astype(BF16)

    def bar_len(seq, row):
        n = jnp.zeros(seq.shape, jnp.int32)
        for s in range(8):
            n = jnp.where(seq == s, cnt_ref[s], n)
        return jnp.clip(n - 64 * row, 0, 64)

    def bar_axis(dim):
        b = iota((1, 128) if dim == 1 else (BARS, 1), dim)
        return b, jnp.where(b < BARS, bar_len(jnp.bitwise_and(b, 7), lax.shift_right_logical(b, 3)), 0)

    def rank_of(seq, row, dim):
        b, lb = bar_axis(dim)
        mine, ml = row * 8 + seq, bar_len(seq, row)
        return count((lb > ml) | ((lb == ml) & (b < mine)), dim), ml

    def depth(kk, dim):
        _, lb = bar_axis(dim)
        return lax.shift_right_logical(jnp.maximum(lb - kk, 0) + 7, 3)

    def ahead(zz, nz, dim):
        return jnp.sum(jnp.minimum(zz, nz).astype(F32), axis=dim, keepdims=True).astype(jnp.int32)

    def slot_code(i, dim):
        seq, row = y * 2 + jnp.bitwise_and(i, 1), lax.shift_right_logical(i, 1)
        rank, ml = rank_of(seq, row, dim)
        before = ahead(jnp.full(i.shape, z, jnp.int32), depth(k, dim), dim)
        code = jnp.bitwise_and(rank + before, 3) * 8 + lax.shift_right_logical(rank, 2)
        return jnp.where((v < ml) & (i < SLOTS), code, -1)

    shape = (NY * ROWS, NK * SP)
    i0 = iota((NY * ROWS, 1), 0)
    o_i = div48(i0)
    ci = div6(i0 - o_i * ROWS)
    ri = i0 - o_i * ROWS - ci * CAPR
    want = jnp.bitwise_and(y + o_i, NY - 1) * 8 + ri
    j0 = iota((1, NK * SP), 1)
    cj = lax.shift_right_logical(j0, 4)
    code_j = slot_code(jnp.bitwise_and(j0, SP - 1), 0)
    pick = onehot(
        (jnp.broadcast_to(ci, shape) == jnp.broadcast_to(cj, shape))
        & (jnp.broadcast_to(want, shape) == jnp.broadcast_to(code_j, shape))
    )
    for h in range(H):
        blocks = jnp.dot(pick, xcat[h], preferred_element_type=F32).astype(BF16)
        for o in range(NY):
            sb[h, o] = blocks[o * ROWS:(o + 1) * ROWS]

    pl.semaphore_wait(barrier, len(partners))

    ycp = {}
    for h in range(H):
        for o in yoffs:
            ycp[h, o] = send(sb.at[h, o], yr.at[h, o], ysend.at[h, o], yrecv.at[h, o], ypart(o))

    def place(i, dim):
        zz = div48(i)
        cc = div6(i - zz * ROWS)
        rr = i - zz * ROWS - cc * CAPR
        nz = depth(k, dim)
        before = ahead(zz, nz, dim)
        live = count(nz > zz, dim)
        rank = 4 * rr + jnp.bitwise_and(y - before, 3)
        p = lax.shift_right_logical(before + rank, 2)
        at = jnp.where(p < LR, cc * LR + p, MAIN + cc * OVR + p - LR)
        return jnp.where(rank < live, at, -1)

    perm1[...] = onehot(jnp.broadcast_to(place(iota((1, GR), 1), 0), (M, GR)) == iota((M, GR), 0))

    zcp = {}
    for h in range(H):
        for o in yoffs:
            ycp[h, o].wait_recv()
        own = sb[h, 0].astype(F32)
        for o in yoffs:
            own = own + yr[h, o].astype(F32)
        g[h, rows(z * ROWS, ROWS), :] = own.astype(BF16)
        for o in zoffs:
            mine = g.at[h, rows(z * ROWS, ROWS)]
            zcp[h, o] = send(mine, mine, zsend.at[h, o], zrecv.at[h, o], zpart(o))

    si = iota((128, 1), 0)
    sa, sbb = lax.shift_right_logical(si, 4), jnp.bitwise_and(lax.shift_right_logical(si, 1), 7)
    swap[...] = onehot(
        jnp.broadcast_to(sbb * 16 + sa * 2 + jnp.bitwise_and(si, 1), (128, 128)) == iota((128, 128), 1)
    )
    perm2[...] = onehot(
        jnp.broadcast_to(place(iota((GR, 1), 0), 1), (GR, M)) == iota((GR, M), 1)
    )
    shape = (NK * SP, NY * ROWS)
    j0 = iota((1, NY * ROWS), 1)
    o_j = div48(j0)
    cj = div6(j0 - o_j * ROWS)
    rj = j0 - o_j * ROWS - cj * CAPR
    have = jnp.bitwise_and(y + NY - o_j, NY - 1) * 8 + rj
    i0 = iota((NK * SP, 1), 0)
    ci = lax.shift_right_logical(i0, 4)
    code_i = slot_code(jnp.bitwise_and(i0, SP - 1), 1)
    back[...] = onehot(
        (jnp.broadcast_to(ci, shape) == jnp.broadcast_to(cj, shape))
        & (jnp.broadcast_to(code_i, shape) == jnp.broadcast_to(have, shape))
    )

    xcp, ccp, vcp, wcp = {}, {}, {}, {}

    def main_at(ln, h):
        return x_v.at[rows(ln * LR, LR), pl.ds(h * DH, DH)]

    def further_at(ln, h):
        return ov_g.at[h, rows(ln * OV, OV)]

    def x_send(ln, h, o, to):
        a, b = main_at(ln, h), further_at(ln, h)
        xcp[h, o] = send(a, a, xsend.at[h, o], xrecv.at[h, o], to)
        vcp[h, o] = send(b, b, vsend.at[h, o], vrecv.at[h, o], to)

    def c_send(ln, h, o):
        a, b = main_at(ln, h), further_at(ln, h)
        ccp[h, o] = send(a, a, csend.at[h, o], crecv.at[h, o], cpart)
        wcp[h, o] = send(b, b, wsend.at[h, o], wrecv.at[h, o], cpart)

    for h in range(H):
        for o in zoffs:
            zcp[h, o].wait_recv()
        lines = jnp.dot(perm1[...], g[h], preferred_element_type=F32).astype(BF16)
        for cc in range(NK):
            ln = slice(h * DH + cc * CW, h * DH + (cc + 1) * CW)
            x_v[rows(line * LR, LR), ln] = lines[cc * LR:(cc + 1) * LR]
        ov_g[h, rows(line * OV, OV)] = lines[MAIN:]
        for o in xoffs:
            x_send(line, h, o, xpart(o))
        c_send(line, h, 0)

    for h in range(H):
        for o in (1, 3, 2):
            xcp[h, o].wait_recv()
            vcp[h, o].wait_recv()
            c_send(c * NX + xo(NX - o), h, o)
        for o in (0, 1, 3, 2):
            ccp[h, o].wait_recv()
            wcp[h, o].wait_recv()
        further = jnp.dot(swap[...], ov_g[h], preferred_element_type=F32).astype(BF16)
        for cc in range(NK):
            x_v[MAIN:, h * DH + cc * CW:h * DH + (cc + 1) * CW] = further[cc * OV:(cc + 1) * OV]
        if h == 0:
            e_copy.wait()

        def mm1(i, carry):
            n = pl.ds(pl.multiple_of(i * 640, 640), 640)
            part = lax.dot_general(
                x_v[:, cols(h)], e_v[n, cols(h)],
                (((1,), (1,)), ((), ())), preferred_element_type=F32,
            )
            l_v[:, n] = part if h == 0 else l_v[:, n] + part
            return carry

        lax.fori_loop(0, V // 640, mm1, 0)

    for start, size in ((0, 128), (128, 128), (MAIN, OV)):
        r = slice(start, start + size)
        t1 = l_v[r, 0:128]
        t2 = jnp.full((size, 128), -jnp.inf, F32)
        for j in range(1, V // 128):
            val = l_v[r, j * 128:(j + 1) * 128]
            t2 = jnp.maximum(t2, jnp.minimum(t1, val))
            t1 = jnp.maximum(t1, val)
        top = jnp.max(t1, axis=1, keepdims=True)
        acc = jnp.zeros((size, 128), F32)
        for j in range(V // 128):
            e = jnp.exp(l_v[r, j * 128:(j + 1) * 128] - top)
            acc = acc + e
            p_v[r, j * 128:(j + 1) * 128] = e.astype(BF16)
        if size < 128:
            pad = jnp.ones((128 - size, 128), F32)
            t1, t2, acc = (jnp.concatenate([a, pad], axis=0) for a in (t1, t2, acc))
        for n, a in enumerate((t1, t2, acc)):
            tt[n, :, start:start + 128] = a.T
    m1, m2, sm = tt[0], tt[1], tt[2]
    n = 128
    while n > 1:
        n //= 2
        a1, b1 = m1[:n], m1[n:]
        m2 = jnp.maximum(jnp.minimum(a1, b1), jnp.maximum(m2[:n], m2[n:]))
        m1 = jnp.maximum(a1, b1)
        sm = sm[:n] + sm[n:]
    loc = m1

    def put(slot, parts):
        for n in range(3):
            st_o[slot, n:n + 1] = parts[n]

    def got3(ref):
        return (ref[0:1], ref[1:2], ref[2:3])

    def spread(ref, factor):
        for i in range(0, ML, 128):
            size = min(128, M - i)
            ref[i:i + size] = jnp.broadcast_to(factor[:, i:i + 128], (128, 128)).T[:size]

    c2, x2, z2, y2 = {}, {}, {}, {}

    def mm2(i):
        n = slice(i * 1024, (i + 1) * 1024)
        obf[:, n] = jnp.dot(p_v[...], e_v[:, n], preferred_element_type=F32).astype(BF16)

    def core_send(h):
        src = obf.at[rows((1 - c) * NX * LR, NX * LR), pl.ds(h * DH, DH)]
        c2[h, 0] = send(src, cr.at[h], c2send.at[h, 0], c2recv.at[h, 0], cpart)
        stack = jnp.concatenate(
            [obf[MAIN:, h * DH + cc * CW:h * DH + (cc + 1) * CW] for cc in range(NK)], axis=0
        )
        ovo[h] = jnp.dot(swap[...], stack, preferred_element_type=F32).astype(BF16)
        src = ovo.at[h, rows((1 - c) * NX * OV, NX * OV)]
        c2[h, 1] = send(src, cro.at[h], c2send.at[h, 1], c2recv.at[h, 1], cpart)

    st_o[...] = jnp.zeros_like(st_o)
    cur = (m1, m2, sm)
    put(0, cur)
    cp = send(st_o.at[0], st_c, scs, scr, cpart)
    mm2(0)
    cp.wait_recv()
    loc2 = st_c[0:1]
    cur = merge([cur, got3(st_c)])
    put(1, cur)
    cps = [send(st_o.at[1], st_x.at[o], sxs.at[o], sxr.at[o], xpart(o)) for o in xoffs]
    mm2(1)
    core_send(0)
    mm2(2)
    for cp in cps:
        cp.wait_recv()
    cur = merge([cur] + [got3(st_x[o]) for o in xoffs])
    put(2, cur)
    scp = [send(st_o.at[2], st_z.at[o], szs.at[o], szr.at[o], zpart(o)) for o in zoffs]
    spread(fsc, jnp.exp(loc - cur[0]))
    spread(fs2, jnp.exp(loc2 - cur[0]))
    mm2(3)
    core_send(1)

    def x2_send(h, o, to):
        x2[h, o] = send(xs.at[h, o], xr.at[h, o], x2send.at[h, o], x2recv.at[h, o], xpart(to))

    def further_factor(ref, ln):
        pair = [ref[pl.ds(MAIN + ln * OVR + e, 1)] for e in range(OVR)]
        return jnp.where(jnp.bitwise_and(iota((OV, 128), 0), 1) == 0, pair[0], pair[1])

    def chip_sum(h, o):
        xx = xo(o)
        ln = c * NX + xx
        at = rows(ln * LR, LR)
        fa, fb = fsc[at], fs2[at]
        for lane in range(0, DH, 128):
            mine = obf[at, h * DH + lane:h * DH + lane + 128].astype(F32)
            theirs = cr[h, rows(xx * LR, LR), lane:lane + 128].astype(F32)
            cc, sub = divmod(lane, CW)
            xs[h, o, cc * LR:(cc + 1) * LR, sub:sub + 128] = (mine * fa + theirs * fb).astype(BF16)
        fa, fb = further_factor(fsc, ln), further_factor(fs2, ln)
        for sub in range(0, CW, 128):
            mine = ovo[h, rows(ln * OV, OV), sub:sub + 128].astype(F32)
            theirs = cro[h, rows(xx * OV, OV), sub:sub + 128].astype(F32)
            xs[h, o, MAIN:, sub:sub + 128] = (mine * fa + theirs * fb).astype(BF16)

    for h in range(H):
        c2[h, 0].wait_recv()
        c2[h, 1].wait_recv()
        for o in (2, 1, 3, 0):
            chip_sum(h, o)
            if o:
                x2_send(h, o, o)

    for cp in scp:
        cp.wait_recv()
    m8 = cur[0]
    m1, m2, sm = merge([cur] + [got3(st_z[o]) for o in zoffs])
    spread(fsc, jnp.exp(m8 - m1) / sm * 64.0)
    margin = (1.0 - jnp.exp(m2 - m1)) / sm
    mg[y] = jnp.broadcast_to(margin, (8, ML))
    mcp = [send(mg.at[y], mg.at[y], ms.at[o], mr.at[o], ypart(o)) for o in yoffs]

    f_main = fsc[rows(line * LR, LR)]
    f_ov = further_factor(fsc, line)

    for h in range(H):
        for o in (1, 3, 2):
            x2[h, o].wait_recv()
        for lane in range(0, CW, 128):
            ln = slice(lane, lane + 128)
            for cc in range(NK + 1):
                r = slice(cc * LR, min(cc * LR + LR, M))
                tot = xs[h, 0, r, ln].astype(F32) + xr[h, 1, r, ln].astype(F32)
                tot = tot + xr[h, 3, r, ln].astype(F32) + xr[h, 2, r, ln].astype(F32)
                pst[r, ln] = (tot * (f_main if cc < NK else f_ov)).astype(BF16)
        zs[h] = jnp.dot(perm2[...], pst[...], preferred_element_type=F32).astype(BF16)
        for o in zoffs:
            src = zs.at[h, rows(lax.rem(z + o, NZ) * ROWS, ROWS)]
            z2[h, o] = send(src, zr.at[h, o], z2send.at[h, o], z2recv.at[h, o], zpart(o))

    for cp in mcp:
        cp.wait_recv()
    lane = iota((1, ML), 1)
    lm = jnp.minimum(lane, M - 1)
    ln = jnp.where(lm < MAIN, lax.shift_right_logical(lm, 5), lax.shift_right_logical(lm - MAIN, 1))
    p = jnp.where(lm < MAIN, jnp.bitwise_and(lm, LR - 1), LR + jnp.bitwise_and(lm, 1))
    kk = jnp.bitwise_and(ln, NX - 1) * NC + lax.shift_right_logical(ln, 2)
    nz = depth(kk, 0)
    befores = [ahead(jnp.full((1, ML), n, jnp.int32), nz, 0) for n in range(NZ + 1)]
    slot = iota((SP, 1), 0)
    rank_i, len_i = rank_of(y * 2 + jnp.bitwise_and(slot, 1), lax.shift_right_logical(slot, 1), 1)
    by_col = jnp.zeros((SP, 64), F32)
    for yy in range(NY):
        gi = 4 * p + yy
        zz = jnp.zeros((1, ML), jnp.int32)
        first = jnp.zeros((1, ML), jnp.int32)
        for n in range(1, NZ):
            past = befores[n] <= gi
            zz = jnp.where(past, n, zz)
            first = jnp.where(past, befores[n], first)
        rank = jnp.where((gi < befores[NZ]) & (lane < M), gi - first, -1)
        vals = jnp.where(
            jnp.broadcast_to(rank, (SP, ML)) == jnp.broadcast_to(rank_i, (SP, ML)),
            jnp.broadcast_to(mg[yy, 0:1], (SP, ML)), 0.0,
        )
        hit = jnp.broadcast_to(zz * NK + kk, (64, ML)) == iota((64, ML), 0)
        by_col = by_col + lax.dot_general(
            vals, jnp.where(hit, 1.0, 0.0), (((1,), (1,)), ((), ())),
            preferred_element_type=F32, precision=lax.Precision.HIGHEST,
        )
    masked = (iota((SP, 64), 1) < len_i) & (iota((SP, 64), 0) < SLOTS)
    by_col = jnp.where(masked, by_col, 0.0)
    wide = (2, 128)
    marg = jnp.zeros(wide, F32)
    for t in range(LEN_DEV):
        target = v * LEN_DEV + t
        for s2 in range(2):
            hit = sum(
                jnp.where(pos_ref[r5, s2:s2 + 1] == target, by_col[2 * r5 + s2:2 * r5 + s2 + 1], 0.0)
                for r5 in range(5)
            )
            val = jnp.broadcast_to(jnp.sum(hit, axis=1, keepdims=True), wide)
            marg = jnp.where((iota(wide, 1) == t) & (iota(wide, 0) == s2), val, marg)
    marg_ref[...] = marg[:, :LEN_DEV]

    for h in range(H):
        for o in zoffs:
            z2[h, o].wait_recv()
        tot = zs[h, rows(z * ROWS, ROWS), :].astype(F32)
        for o in zoffs:
            tot = tot + zr[h, o].astype(F32)
        ys[h] = tot.astype(BF16)
        yr2[h, 0] = ys[h]
        for o in yoffs:
            y2[h, o] = send(ys.at[h], yr2.at[h, o], y2send.at[h, o], y2recv.at[h, o], ypart(o))

    for h in range(H):
        for o in yoffs:
            y2[h, o].wait_recv()
        cat = jnp.concatenate([yr2[h, o] for o in range(NY)], axis=0)
        got = jnp.dot(back[...], cat, preferred_element_type=F32)
        for cc in range(NK):
            res[:, h * DH + cc * CW:h * DH + (cc + 1) * CW] = got[cc * SP:(cc + 1) * SP]
    for i in range(5):
        out_ref[i] = res[2 * i:2 * i + 2].astype(BF16)
    for cp in pending:
        cp.wait_send()


def readout(q, sc, gain, table, counts, positions):
    dma = pltpu.SemaphoreType.DMA
    vm = pl.BlockSpec(memory_space=pltpu.VMEM)
    return pl.pallas_call(
        kernel,
        out_shape=(
            jax.ShapeDtypeStruct(q.shape, BF16),
            jax.ShapeDtypeStruct((2, LEN_DEV), F32),
        ),
        in_specs=[
            vm, vm, vm, pl.BlockSpec(memory_space=pl.ANY), pl.BlockSpec(memory_space=pltpu.SMEM), vm
        ],
        out_specs=(vm, vm),
        scratch_shapes=[
            pltpu.VMEM((V, D), BF16),
            pltpu.VMEM((SP, D), F32),
            pltpu.VMEM((SP, D // 128), F32),
            pltpu.VMEM((H, NK * SP, CW), BF16),
            pltpu.VMEM((H, NY, ROWS, CW), BF16),
            pltpu.VMEM((H, NY, ROWS, CW), BF16),
            pltpu.VMEM((H, GR, CW), BF16),
            pltpu.VMEM((M, GR), BF16),
            pltpu.VMEM((GR, M), BF16),
            pltpu.VMEM((128, 128), BF16),
            pltpu.VMEM((NK * SP, NY * ROWS), BF16),
            pltpu.VMEM((M, D), BF16),
            pltpu.VMEM((H, NK * OV, CW), BF16),
            pltpu.VMEM((M, V), F32),
            pltpu.VMEM((M, V), BF16),
            pltpu.VMEM((3, 128, ML), F32),
            pltpu.VMEM((M, 128), F32),
            pltpu.VMEM((M, 128), F32),
            pltpu.VMEM((M, D), BF16),
            pltpu.VMEM((H, NK * OV, CW), BF16),
            pltpu.VMEM((H, NX * LR, DH), BF16),
            pltpu.VMEM((H, NX * OV, CW), BF16),
            pltpu.VMEM((H, NX, M, CW), BF16),
            pltpu.VMEM((H, NX, M, CW), BF16),
            pltpu.VMEM((M, CW), BF16),
            pltpu.VMEM((H, GR, CW), BF16),
            pltpu.VMEM((H, NZ, ROWS, CW), BF16),
            pltpu.VMEM((H, ROWS, CW), BF16),
            pltpu.VMEM((H, NY, ROWS, CW), BF16),
            pltpu.VMEM((SP, D), F32),
            pltpu.VMEM((NY, 8, ML), F32),
            pltpu.VMEM((8, ML), F32),
            pltpu.VMEM((NX, 8, ML), F32),
            pltpu.VMEM((NZ, 8, ML), F32),
            pltpu.VMEM((3, 8, ML), F32),
            dma,
            dma((H, NY)), dma((H, NY)), dma((H, NZ)), dma((H, NZ)),
            dma((H, NX)), dma((H, NX)), dma((H, NX)), dma((H, NX)),
            dma((H, NX)), dma((H, NX)), dma((H, NX)), dma((H, NX)),
            dma((H, 2)), dma((H, 2)), dma((H, NX)), dma((H, NX)),
            dma((H, NZ)), dma((H, NZ)), dma((H, NY)), dma((H, NY)),
            dma, dma, dma((NX,)), dma((NX,)), dma((NZ,)), dma((NZ,)), dma((NY,)), dma((NY,)),
        ],
        compiler_params=pltpu.CompilerParams(
            collective_id=0, has_side_effects=True, vmem_limit_bytes=60 << 20
        ),
        cost_estimate=pl.CostEstimate(
            flops=4 * M * V * D, bytes_accessed=2 * V * D, transcendentals=M * V
        ),
        name="readout",
    )(q, sc, gain, table, counts, positions)


def on_device(quantized, scales, norm_gain, embed_table, counts, positions):
    expected, margins = readout(
        quantized[0], scales[0], norm_gain.reshape(1, D), embed_table, counts,
        positions.transpose(1, 2, 0),
    )
    return (expected[None], margins)


def solution(mesh):
    in_specs = (
        P("vocab", None, "pos", None),
        P("vocab", None, "pos", None),
        P(),
        P("vocab", None),
        P(),
        P(None, None, "pos"),
    )
    out_specs = (P("vocab", None, "pos", None), P("pos", "vocab"))
    return jax.shard_map(
        on_device, mesh=mesh, in_specs=in_specs, out_specs=out_specs, check_vma=False
    )
```

```python
import functools

import jax
import jax.numpy as jnp
from jax import lax
from jax.experimental import pallas as pl
from jax.experimental.pallas import tpu as pltpu
from jax.sharding import PartitionSpec as P

MESH = pl.DeviceIdType.MESH
F32 = jnp.float32
BF16 = jnp.bfloat16

D = 4096
LEN_DEV = 10
NY, NZ, NX, NC = 4, 8, 4, 2
NK = NX * NC
CAPR = 6
ROWS = NK * CAPR
GR = NZ * ROWS
LR = 32
OVR = 2
MAIN = NK * LR
OV = NK * OVR
M = MAIN + OV
ML = 384
V = 1280
H = 4
DH = D // H
CW = DH // NK
SLOTS = 10
SP = 16
BARS = 40


def onehot(cond):
    return jnp.where(cond, 1.0, 0.0).astype(BF16)


def iota(shape, dim):
    return lax.broadcasted_iota(jnp.int32, shape, dim)


def div48(i):
    return lax.shift_right_logical(i * 683, 15)


def div6(i):
    return lax.shift_right_logical(i * 43, 8)


def count(cond, axis):
    return jnp.sum(jnp.where(cond, 1.0, 0.0), axis=axis, keepdims=True).astype(jnp.int32)


def merge(parts):
    top = functools.reduce(jnp.maximum, [p[0] for p in parts])
    total = sum(p[2] * jnp.exp(p[0] - top) for p in parts)
    m1, m2 = parts[0][0], parts[0][1]
    for p in parts[1:]:
        m2 = jnp.maximum(jnp.minimum(m1, p[0]), jnp.maximum(m2, p[1]))
        m1 = jnp.maximum(m1, p[0])
    return m1, m2, total


def kernel(
    q_ref, sc_ref, gain_ref, e_hbm, cnt_ref, pos_ref,
    out_ref, marg_ref,
    e_v, qf, sf, xcat, sb, yr, g, perm1, perm2, swap, back, x_v, ov_g, l_v, p_v, tt, fsc, fs2, fx, obf,
    ovo, cr, cro, xs, xr, pst, zs, zr, ys, yr2, res, mg, st_c, st_x, st_z, st_o,
    esem, ysend, yrecv, zsend, zrecv, xsend, xrecv, csend, crecv,
    vsend, vrecv, wsend, wrecv,
    c2send, c2recv, x2send, x2recv, z2send, z2recv, y2send, y2recv,
    scs, scr, sxs, sxr, szs, szr, ms, mr,
):
    y = lax.axis_index("pos")
    v = lax.axis_index("vocab")
    z = v // NK
    k = lax.rem(v, NK)
    x = k // NC
    c = lax.rem(k, NC)
    line = c * NX + x

    def dev(yy, zz, xx, cc):
        return (yy, zz * NK + xx * NC + cc)

    def xo(o):
        return lax.rem(x + o, NX)

    def ypart(o):
        return dev(lax.rem(y + o, NY), z, x, c)

    def zpart(o):
        return dev(y, lax.rem(z + o, NZ), x, c)

    def xpart(o):
        return dev(y, z, xo(o), c)

    cpart = dev(y, z, x, 1 - c)
    yoffs, zoffs, xoffs = (1, 3, 2), (4, 3, 5, 2, 6, 1, 7), (2, 1, 3)
    pending = []

    def send(src, dst, ss, rs, to):
        cp = pltpu.make_async_remote_copy(
            src_ref=src, dst_ref=dst, send_sem=ss, recv_sem=rs, device_id=to, device_id_type=MESH
        )
        cp.start()
        pending.append(cp)
        return cp

    def rows(start, size):
        return pl.ds(pl.multiple_of(start, 16), size)

    def cols(h):
        return slice(h * DH, (h + 1) * DH)

    barrier = pltpu.get_barrier_semaphore()
    partners = [ypart(o) for o in yoffs] + [zpart(o) for o in zoffs]
    partners += [xpart(o) for o in xoffs] + [cpart]
    for to in partners:
        pl.semaphore_signal(barrier, inc=1, device_id=to, device_id_type=MESH)
    e_copy = pltpu.make_async_copy(e_hbm, e_v, esem)
    e_copy.start()

    for i in range(5):
        qf[2 * i:2 * i + 2] = q_ref[i].astype(F32)
        sf[2 * i:2 * i + 2] = sc_ref[i]
    deq = [qf[:SLOTS, i * 128:(i + 1) * 128] * sf[:SLOTS, i:i + 1] for i in range(D // 128)]
    sq = sum(d * d for d in deq)
    inv = lax.rsqrt(jnp.sum(sq, axis=1, keepdims=True) * (1.0 / D) + 1e-6)
    xcat[...] = jnp.zeros_like(xcat)
    for i in range(D // 128):
        h, rest = divmod(i * 128, DH)
        cc, lane = divmod(rest, CW)
        gn = gain_ref[:, i * 128:(i + 1) * 128]
        xcat[h, cc * SP:cc * SP + SLOTS, lane:lane + 128] = (deq[i] * inv * gn).astype(BF16)

    def bar_len(seq, row):
        n = jnp.zeros(seq.shape, jnp.int32)
        for s in range(8):
            n = jnp.where(seq == s, cnt_ref[s], n)
        return jnp.clip(n - 64 * row, 0, 64)

    def bar_axis(dim):
        b = iota((1, 128) if dim == 1 else (BARS, 1), dim)
        return b, jnp.where(b < BARS, bar_len(jnp.bitwise_and(b, 7), lax.shift_right_logical(b, 3)), 0)

    def rank_of(seq, row, dim):
        b, lb = bar_axis(dim)
        mine, ml = row * 8 + seq, bar_len(seq, row)
        return count((lb > ml) | ((lb == ml) & (b < mine)), dim), ml

    def depth(kk, dim):
        _, lb = bar_axis(dim)
        return lax.shift_right_logical(jnp.maximum(lb - kk, 0) + 7, 3)

    def ahead(zz, nz, dim):
        return jnp.sum(jnp.minimum(zz, nz).astype(F32), axis=dim, keepdims=True).astype(jnp.int32)

    def slot_code(i, dim):
        seq, row = y * 2 + jnp.bitwise_and(i, 1), lax.shift_right_logical(i, 1)
        rank, ml = rank_of(seq, row, dim)
        before = ahead(jnp.full(i.shape, z, jnp.int32), depth(k, dim), dim)
        code = jnp.bitwise_and(rank + before, 3) * 8 + lax.shift_right_logical(rank, 2)
        return jnp.where((v < ml) & (i < SLOTS), code, -1)

    shape = (NY * ROWS, NK * SP)
    i0 = iota((NY * ROWS, 1), 0)
    o_i = div48(i0)
    ci = div6(i0 - o_i * ROWS)
    ri = i0 - o_i * ROWS - ci * CAPR
    want = jnp.bitwise_and(y + o_i, NY - 1) * 8 + ri
    j0 = iota((1, NK * SP), 1)
    cj = lax.shift_right_logical(j0, 4)
    code_j = slot_code(jnp.bitwise_and(j0, SP - 1), 0)
    pick = onehot(
        (jnp.broadcast_to(ci, shape) == jnp.broadcast_to(cj, shape))
        & (jnp.broadcast_to(want, shape) == jnp.broadcast_to(code_j, shape))
    )
    for h in range(H):
        blocks = jnp.dot(pick, xcat[h], preferred_element_type=F32).astype(BF16)
        for o in range(NY):
            sb[h, o] = blocks[o * ROWS:(o + 1) * ROWS]

    pl.semaphore_wait(barrier, len(partners))

    ycp = {}
    for h in range(H):
        for o in yoffs:
            ycp[h, o] = send(sb.at[h, o], yr.at[h, o], ysend.at[h, o], yrecv.at[h, o], ypart(o))

    def place(i, dim):
        zz = div48(i)
        cc = div6(i - zz * ROWS)
        rr = i - zz * ROWS - cc * CAPR
        nz = depth(k, dim)
        before = ahead(zz, nz, dim)
        live = count(nz > zz, dim)
        rank = 4 * rr + jnp.bitwise_and(y - before, 3)
        p = lax.shift_right_logical(before + rank, 2)
        at = jnp.where(p < LR, cc * LR + p, MAIN + cc * OVR + p - LR)
        return jnp.where(rank < live, at, -1)

    perm1[...] = onehot(jnp.broadcast_to(place(iota((1, GR), 1), 0), (M, GR)) == iota((M, GR), 0))

    zcp = {}
    for h in range(H):
        for o in yoffs:
            ycp[h, o].wait_recv()
        own = sb[h, 0].astype(F32)
        for o in yoffs:
            own = own + yr[h, o].astype(F32)
        g[h, rows(z * ROWS, ROWS), :] = own.astype(BF16)
        for o in zoffs:
            mine = g.at[h, rows(z * ROWS, ROWS)]
            zcp[h, o] = send(mine, mine, zsend.at[h, o], zrecv.at[h, o], zpart(o))

    si = iota((128, 1), 0)
    sa, sbb = lax.shift_right_logical(si, 4), jnp.bitwise_and(lax.shift_right_logical(si, 1), 7)
    swap[...] = onehot(
        jnp.broadcast_to(sbb * 16 + sa * 2 + jnp.bitwise_and(si, 1), (128, 128)) == iota((128, 128), 1)
    )
    perm2[...] = onehot(
        jnp.broadcast_to(place(iota((GR, 1), 0), 1), (GR, M)) == iota((GR, M), 1)
    )
    shape = (NK * SP, NY * ROWS)
    j0 = iota((1, NY * ROWS), 1)
    o_j = div48(j0)
    cj = div6(j0 - o_j * ROWS)
    rj = j0 - o_j * ROWS - cj * CAPR
    have = jnp.bitwise_and(y + NY - o_j, NY - 1) * 8 + rj
    i0 = iota((NK * SP, 1), 0)
    ci = lax.shift_right_logical(i0, 4)
    code_i = slot_code(jnp.bitwise_and(i0, SP - 1), 1)
    back[...] = onehot(
        (jnp.broadcast_to(ci, shape) == jnp.broadcast_to(cj, shape))
        & (jnp.broadcast_to(code_i, shape) == jnp.broadcast_to(have, shape))
    )

    xcp, ccp, vcp, wcp = {}, {}, {}, {}

    def main_at(ln, h):
        return x_v.at[rows(ln * LR, LR), pl.ds(h * DH, DH)]

    def further_at(ln, h):
        return ov_g.at[h, rows(ln * OV, OV)]

    def x_send(ln, h, o, to):
        a, b = main_at(ln, h), further_at(ln, h)
        xcp[h, o] = send(a, a, xsend.at[h, o], xrecv.at[h, o], to)
        vcp[h, o] = send(b, b, vsend.at[h, o], vrecv.at[h, o], to)

    def c_send(ln, h, o):
        a, b = main_at(ln, h), further_at(ln, h)
        ccp[h, o] = send(a, a, csend.at[h, o], crecv.at[h, o], cpart)
        wcp[h, o] = send(b, b, wsend.at[h, o], wrecv.at[h, o], cpart)

    for h in range(H):
        for o in zoffs:
            zcp[h, o].wait_recv()
        lines = jnp.dot(perm1[...], g[h], preferred_element_type=F32).astype(BF16)
        for cc in range(NK):
            ln = slice(h * DH + cc * CW, h * DH + (cc + 1) * CW)
            x_v[rows(line * LR, LR), ln] = lines[cc * LR:(cc + 1) * LR]
        ov_g[h, rows(line * OV, OV)] = lines[MAIN:]
        for o in xoffs:
            x_send(line, h, o, xpart(o))
        c_send(line, h, 0)

    def mm1(h):
        for o in (0, 1, 3, 2):
            ccp[h, o].wait_recv()
            wcp[h, o].wait_recv()
        further = jnp.dot(swap[...], ov_g[h], preferred_element_type=F32).astype(BF16)
        for cc in range(NK):
            x_v[MAIN:, h * DH + cc * CW:h * DH + (cc + 1) * CW] = further[cc * OV:(cc + 1) * OV]
        if h == 0:
            e_copy.wait()

        def body(i, carry):
            n = pl.ds(pl.multiple_of(i * 640, 640), 640)
            part = lax.dot_general(
                x_v[:, cols(h)], e_v[n, cols(h)],
                (((1,), (1,)), ((), ())), preferred_element_type=F32,
            )
            l_v[:, n] = part if h == 0 else l_v[:, n] + part
            return carry

        lax.fori_loop(0, V // 640, body, 0)

    for h in range(H):
        for o in (1, 3, 2):
            xcp[h, o].wait_recv()
            vcp[h, o].wait_recv()
            c_send(c * NX + xo(NX - o), h, o)
        if h:
            mm1(h - 1)
    mm1(H - 1)

    for start, size in ((0, 128), (128, 128), (MAIN, OV)):
        r = slice(start, start + size)
        t1 = l_v[r, 0:128]
        t2 = jnp.full((size, 128), -jnp.inf, F32)
        for j in range(1, V // 128):
            val = l_v[r, j * 128:(j + 1) * 128]
            t2 = jnp.maximum(t2, jnp.minimum(t1, val))
            t1 = jnp.maximum(t1, val)
        top = jnp.max(t1, axis=1, keepdims=True)
        acc = jnp.zeros((size, 128), F32)
        for j in range(V // 128):
            e = jnp.exp(l_v[r, j * 128:(j + 1) * 128] - top)
            acc = acc + e
            p_v[r, j * 128:(j + 1) * 128] = e.astype(BF16)
        if size < 128:
            pad = jnp.ones((128 - size, 128), F32)
            t1, t2, acc = (jnp.concatenate([a, pad], axis=0) for a in (t1, t2, acc))
        for n, a in enumerate((t1, t2, acc)):
            tt[n, :, start:start + 128] = a.T
    m1, m2, sm = tt[0], tt[1], tt[2]
    n = 128
    while n > 1:
        n //= 2
        a1, b1 = m1[:n], m1[n:]
        m2 = jnp.maximum(jnp.minimum(a1, b1), jnp.maximum(m2[:n], m2[n:]))
        m1 = jnp.maximum(a1, b1)
        sm = sm[:n] + sm[n:]
    loc = m1

    def put(slot, parts):
        for n in range(3):
            st_o[slot, n:n + 1] = parts[n]

    def got3(ref):
        return (ref[0:1], ref[1:2], ref[2:3])

    def spread(ref, factor):
        for i in range(0, ML, 128):
            size = min(128, M - i)
            ref[i:i + size] = jnp.broadcast_to(factor[:, i:i + 128], (128, 128)).T[:size]

    c2, x2, z2, y2 = {}, {}, {}, {}

    def mm2(h):
        obf[:, cols(h)] = jnp.dot(p_v[...], e_v[:, cols(h)], preferred_element_type=F32).astype(BF16)

    def core_send(h):
        src = obf.at[rows((1 - c) * NX * LR, NX * LR), pl.ds(h * DH, DH)]
        c2[h, 0] = send(src, cr.at[h], c2send.at[h, 0], c2recv.at[h, 0], cpart)
        stack = jnp.concatenate(
            [obf[MAIN:, h * DH + cc * CW:h * DH + (cc + 1) * CW] for cc in range(NK)], axis=0
        )
        ovo[h] = jnp.dot(swap[...], stack, preferred_element_type=F32).astype(BF16)
        src = ovo.at[h, rows((1 - c) * NX * OV, NX * OV)]
        c2[h, 1] = send(src, cro.at[h], c2send.at[h, 1], c2recv.at[h, 1], cpart)

    st_o[...] = jnp.zeros_like(st_o)
    cur = (m1, m2, sm)
    put(0, cur)
    cp = send(st_o.at[0], st_c, scs, scr, cpart)
    mm2(0)
    cp.wait_recv()
    loc2 = st_c[0:1]
    cur = merge([cur, got3(st_c)])
    chip = cur[0]
    put(1, cur)
    xst = [send(st_o.at[1], st_x.at[o], sxs.at[o], sxr.at[o], xpart(o)) for o in xoffs]
    core_send(0)
    spread(fsc, jnp.exp(loc - chip))
    spread(fs2, jnp.exp(loc2 - chip))

    def x2_send(h, o, to):
        x2[h, o] = send(xs.at[h, o], xr.at[h, o], x2send.at[h, o], x2recv.at[h, o], xpart(to))

    def further_factor(ref, ln):
        pair = [ref[pl.ds(MAIN + ln * OVR + e, 1)] for e in range(OVR)]
        return jnp.where(jnp.bitwise_and(iota((OV, 128), 0), 1) == 0, pair[0], pair[1])

    def chip_sum(h, o):
        xx = xo(o)
        ln = c * NX + xx
        at = rows(ln * LR, LR)
        fa, fb = fsc[at], fs2[at]
        for lane in range(0, DH, 128):
            mine = obf[at, h * DH + lane:h * DH + lane + 128].astype(F32)
            theirs = cr[h, rows(xx * LR, LR), lane:lane + 128].astype(F32)
            cc, sub = divmod(lane, CW)
            xs[h, o, cc * LR:(cc + 1) * LR, sub:sub + 128] = (mine * fa + theirs * fb).astype(BF16)
        fa, fb = further_factor(fsc, ln), further_factor(fs2, ln)
        for sub in range(0, CW, 128):
            mine = ovo[h, rows(ln * OV, OV), sub:sub + 128].astype(F32)
            theirs = cro[h, rows(xx * OV, OV), sub:sub + 128].astype(F32)
            xs[h, o, MAIN:, sub:sub + 128] = (mine * fa + theirs * fb).astype(BF16)

    def chip_sums(h):
        c2[h, 0].wait_recv()
        c2[h, 1].wait_recv()
        for o in (2, 1, 3, 0):
            chip_sum(h, o)
            if o:
                x2_send(h, o, o)

    for h in range(1, H):
        mm2(h)
        core_send(h)
        chip_sums(h - 1)
    chip_sums(H - 1)

    for cp in xst:
        cp.wait_recv()
    cur = merge([cur] + [got3(st_x[o]) for o in xoffs])
    put(2, cur)
    zst = [send(st_o.at[2], st_z.at[o], szs.at[o], szr.at[o], zpart(o)) for o in zoffs]
    for cp in zst:
        cp.wait_recv()
    m1, m2, sm = merge([cur] + [got3(st_z[o]) for o in zoffs])
    for o in range(NX):
        spread(fx.at[o], jnp.exp((st_x[o, 0:1] if o else chip) - m1) / sm * 64.0)
    margin = (1.0 - jnp.exp(m2 - m1)) / sm
    mg[y] = jnp.broadcast_to(margin, (8, ML))
    mcp = [send(mg.at[y], mg.at[y], ms.at[o], mr.at[o], ypart(o)) for o in yoffs]

    f_main = [fx[o, rows(line * LR, LR)] for o in range(NX)]
    f_ov = [further_factor(fx.at[o], line) for o in range(NX)]

    for h in range(H):
        for o in (1, 3, 2):
            x2[h, o].wait_recv()
        for lane in range(0, CW, 128):
            ln = slice(lane, lane + 128)
            for cc in range(NK + 1):
                r = slice(cc * LR, min(cc * LR + LR, M))
                f = f_main if cc < NK else f_ov
                tot = xs[h, 0, r, ln].astype(F32) * f[0]
                for o in xoffs:
                    tot = tot + xr[h, o, r, ln].astype(F32) * f[o]
                pst[r, ln] = tot.astype(BF16)
        zs[h] = jnp.dot(perm2[...], pst[...], preferred_element_type=F32).astype(BF16)
        for o in zoffs:
            src = zs.at[h, rows(lax.rem(z + o, NZ) * ROWS, ROWS)]
            z2[h, o] = send(src, zr.at[h, o], z2send.at[h, o], z2recv.at[h, o], zpart(o))

    for cp in mcp:
        cp.wait_recv()
    lane = iota((1, ML), 1)
    lm = jnp.minimum(lane, M - 1)
    ln = jnp.where(lm < MAIN, lax.shift_right_logical(lm, 5), lax.shift_right_logical(lm - MAIN, 1))
    p = jnp.where(lm < MAIN, jnp.bitwise_and(lm, LR - 1), LR + jnp.bitwise_and(lm, 1))
    kk = jnp.bitwise_and(ln, NX - 1) * NC + lax.shift_right_logical(ln, 2)
    nz = depth(kk, 0)
    befores = [ahead(jnp.full((1, ML), n, jnp.int32), nz, 0) for n in range(NZ + 1)]
    slot = iota((SP, 1), 0)
    rank_i, len_i = rank_of(y * 2 + jnp.bitwise_and(slot, 1), lax.shift_right_logical(slot, 1), 1)
    by_col = jnp.zeros((SP, 64), F32)
    for yy in range(NY):
        gi = 4 * p + yy
        zz = jnp.zeros((1, ML), jnp.int32)
        first = jnp.zeros((1, ML), jnp.int32)
        for n in range(1, NZ):
            past = befores[n] <= gi
            zz = jnp.where(past, n, zz)
            first = jnp.where(past, befores[n], first)
        rank = jnp.where((gi < befores[NZ]) & (lane < M), gi - first, -1)
        vals = jnp.where(
            jnp.broadcast_to(rank, (SP, ML)) == jnp.broadcast_to(rank_i, (SP, ML)),
            jnp.broadcast_to(mg[yy, 0:1], (SP, ML)), 0.0,
        )
        hit = jnp.broadcast_to(zz * NK + kk, (64, ML)) == iota((64, ML), 0)
        by_col = by_col + lax.dot_general(
            vals, jnp.where(hit, 1.0, 0.0), (((1,), (1,)), ((), ())),
            preferred_element_type=F32, precision=lax.Precision.HIGHEST,
        )
    masked = (iota((SP, 64), 1) < len_i) & (iota((SP, 64), 0) < SLOTS)
    by_col = jnp.where(masked, by_col, 0.0)
    wide = (2, 128)
    marg = jnp.zeros(wide, F32)
    for t in range(LEN_DEV):
        target = v * LEN_DEV + t
        for s2 in range(2):
            hit = sum(
                jnp.where(pos_ref[r5, s2:s2 + 1] == target, by_col[2 * r5 + s2:2 * r5 + s2 + 1], 0.0)
                for r5 in range(5)
            )
            val = jnp.broadcast_to(jnp.sum(hit, axis=1, keepdims=True), wide)
            marg = jnp.where((iota(wide, 1) == t) & (iota(wide, 0) == s2), val, marg)
    marg_ref[...] = marg[:, :LEN_DEV]

    for h in range(H):
        for o in zoffs:
            z2[h, o].wait_recv()
        tot = zs[h, rows(z * ROWS, ROWS), :].astype(F32)
        for o in zoffs:
            tot = tot + zr[h, o].astype(F32)
        ys[h] = tot.astype(BF16)
        yr2[h, 0] = ys[h]
        for o in yoffs:
            y2[h, o] = send(ys.at[h], yr2.at[h, o], y2send.at[h, o], y2recv.at[h, o], ypart(o))

    for h in range(H):
        for o in yoffs:
            y2[h, o].wait_recv()
        cat = jnp.concatenate([yr2[h, o] for o in range(NY)], axis=0)
        got = jnp.dot(back[...], cat, preferred_element_type=F32)
        for cc in range(NK):
            res[:, h * DH + cc * CW:h * DH + (cc + 1) * CW] = got[cc * SP:(cc + 1) * SP]
    for i in range(5):
        out_ref[i] = res[2 * i:2 * i + 2].astype(BF16)
    for cp in pending:
        cp.wait_send()


def readout(q, sc, gain, table, counts, positions):
    dma = pltpu.SemaphoreType.DMA
    vm = pl.BlockSpec(memory_space=pltpu.VMEM)
    return pl.pallas_call(
        kernel,
        out_shape=(
            jax.ShapeDtypeStruct(q.shape, BF16),
            jax.ShapeDtypeStruct((2, LEN_DEV), F32),
        ),
        in_specs=[
            vm, vm, vm, pl.BlockSpec(memory_space=pl.ANY), pl.BlockSpec(memory_space=pltpu.SMEM), vm
        ],
        out_specs=(vm, vm),
        scratch_shapes=[
            pltpu.VMEM((V, D), BF16),
            pltpu.VMEM((SP, D), F32),
            pltpu.VMEM((SP, D // 128), F32),
            pltpu.VMEM((H, NK * SP, CW), BF16),
            pltpu.VMEM((H, NY, ROWS, CW), BF16),
            pltpu.VMEM((H, NY, ROWS, CW), BF16),
            pltpu.VMEM((H, GR, CW), BF16),
            pltpu.VMEM((M, GR), BF16),
            pltpu.VMEM((GR, M), BF16),
            pltpu.VMEM((128, 128), BF16),
            pltpu.VMEM((NK * SP, NY * ROWS), BF16),
            pltpu.VMEM((M, D), BF16),
            pltpu.VMEM((H, NK * OV, CW), BF16),
            pltpu.VMEM((M, V), F32),
            pltpu.VMEM((M, V), BF16),
            pltpu.VMEM((3, 128, ML), F32),
            pltpu.VMEM((M, 128), F32),
            pltpu.VMEM((M, 128), F32),
            pltpu.VMEM((NX, M, 128), F32),
            pltpu.VMEM((M, D), BF16),
            pltpu.VMEM((H, NK * OV, CW), BF16),
            pltpu.VMEM((H, NX * LR, DH), BF16),
            pltpu.VMEM((H, NX * OV, CW), BF16),
            pltpu.VMEM((H, NX, M, CW), BF16),
            pltpu.VMEM((H, NX, M, CW), BF16),
            pltpu.VMEM((M, CW), BF16),
            pltpu.VMEM((H, GR, CW), BF16),
            pltpu.VMEM((H, NZ, ROWS, CW), BF16),
            pltpu.VMEM((H, ROWS, CW), BF16),
            pltpu.VMEM((H, NY, ROWS, CW), BF16),
            pltpu.VMEM((SP, D), F32),
            pltpu.VMEM((NY, 8, ML), F32),
            pltpu.VMEM((8, ML), F32),
            pltpu.VMEM((NX, 8, ML), F32),
            pltpu.VMEM((NZ, 8, ML), F32),
            pltpu.VMEM((3, 8, ML), F32),
            dma,
            dma((H, NY)), dma((H, NY)), dma((H, NZ)), dma((H, NZ)),
            dma((H, NX)), dma((H, NX)), dma((H, NX)), dma((H, NX)),
            dma((H, NX)), dma((H, NX)), dma((H, NX)), dma((H, NX)),
            dma((H, 2)), dma((H, 2)), dma((H, NX)), dma((H, NX)),
            dma((H, NZ)), dma((H, NZ)), dma((H, NY)), dma((H, NY)),
            dma, dma, dma((NX,)), dma((NX,)), dma((NZ,)), dma((NZ,)), dma((NY,)), dma((NY,)),
        ],
        compiler_params=pltpu.CompilerParams(
            collective_id=0, has_side_effects=True, vmem_limit_bytes=60 << 20
        ),
        cost_estimate=pl.CostEstimate(
            flops=4 * M * V * D, bytes_accessed=2 * V * D, transcendentals=M * V
        ),
        name="readout",
    )(q, sc, gain, table, counts, positions)


def hand_out(a, b, out_a, out_b):
    out_a[...] = a[...]
    out_b[...] = b[...]


def on_device(quantized, scales, norm_gain, embed_table, counts, positions):
    expected, margins = readout(
        quantized[0], scales[0], norm_gain.reshape(1, D), embed_table, counts,
        positions.transpose(1, 2, 0),
    )
    vm = pl.BlockSpec(memory_space=pltpu.VMEM)
    expected, margins = pl.pallas_call(
        hand_out,
        out_shape=tuple(jax.ShapeDtypeStruct(a.shape, a.dtype) for a in (expected, margins)),
        in_specs=[vm, vm], out_specs=(vm, vm), name="hand_out",
    )(expected, margins)
    return (expected[None], margins)


def solution(mesh):
    in_specs = (
        P("vocab", None, "pos", None),
        P("vocab", None, "pos", None),
        P(),
        P("vocab", None),
        P(),
        P(None, None, "pos"),
    )
    out_specs = (P("vocab", None, "pos", None), P("pos", "vocab"))
    return jax.shard_map(
        on_device, mesh=mesh, in_specs=in_specs, out_specs=out_specs, check_vma=False
    )
```

```python
import functools

import jax
import jax.numpy as jnp
from jax import lax
from jax.experimental import pallas as pl
from jax.experimental.pallas import tpu as pltpu
from jax.sharding import PartitionSpec as P

MESH = pl.DeviceIdType.MESH
F32 = jnp.float32
BF16 = jnp.bfloat16

D = 4096
LEN_DEV = 10
NY, NZ, NX, NC = 4, 8, 4, 2
NK = NX * NC
CAPR = 6
ROWS = NK * CAPR
GR = NZ * ROWS
LR = 32
OVR = 2
MAIN = NK * LR
OV = NK * OVR
M = MAIN + OV
ML = 384
V = 1280
H = 4
DH = D // H
CW = DH // NK
SLOTS = 10
SP = 16
BARS = 40
Y_OUT = ((0, 1), (1, 4))
Z_OUT = ((0, 1), (1, 2), (2, 3), (3, 4))
Z_BACK = ((0, 1), (1, 2), (2, 3), (3, 4))
Y_BACK = ((0, 3), (3, 4))


def onehot(cond):
    return jnp.where(cond, 1.0, 0.0).astype(BF16)


def iota(shape, dim):
    return lax.broadcasted_iota(jnp.int32, shape, dim)


def div48(i):
    return lax.shift_right_logical(i * 683, 15)


def div6(i):
    return lax.shift_right_logical(i * 43, 8)


def count(cond, axis):
    return jnp.sum(jnp.where(cond, 1.0, 0.0), axis=axis, keepdims=True).astype(jnp.int32)


def merge(parts):
    top = functools.reduce(jnp.maximum, [p[0] for p in parts])
    total = sum(p[2] * jnp.exp(p[0] - top) for p in parts)
    m1, m2 = parts[0][0], parts[0][1]
    for p in parts[1:]:
        m2 = jnp.maximum(jnp.minimum(m1, p[0]), jnp.maximum(m2, p[1]))
        m1 = jnp.maximum(m1, p[0])
    return m1, m2, total


def kernel(
    q_ref, sc_ref, gain_ref, e_hbm, cnt_ref, pos_ref,
    out_ref, marg_ref,
    e_v, qf, sf, xcat, sb, yr, g, perm1, perm2, swap, back, x_v, lg, l_v, p_v, tt, fsc, fs2, fx, obf,
    ovo, cr, cro, xs, xr, pst, zs, zr, yr2, res, mg, st_c, st_x, st_z, st_o,
    esem, ysend, yrecv, zsend, zrecv, xsend, xrecv, csend, crecv,
    c2send, c2recv, x2send, x2recv, z2send, z2recv, y2send, y2recv,
    scs, scr, sxs, sxr, szs, szr, ms, mr,
):
    y = lax.axis_index("pos")
    v = lax.axis_index("vocab")
    z = v // NK
    k = lax.rem(v, NK)
    x = k // NC
    c = lax.rem(k, NC)
    line = c * NX + x

    def dev(yy, zz, xx, cc):
        return (yy, zz * NK + xx * NC + cc)

    def xo(o):
        return lax.rem(x + o, NX)

    def ypart(o):
        return dev(lax.rem(y + o, NY), z, x, c)

    def zpart(o):
        return dev(y, lax.rem(z + o, NZ), x, c)

    def xpart(o):
        return dev(y, z, xo(o), c)

    cpart = dev(y, z, x, 1 - c)
    yoffs, zoffs, xoffs = (1, 3, 2), (4, 3, 5, 2, 6, 1, 7), (2, 1, 3)
    pending = []

    def send(src, dst, ss, rs, to):
        cp = pltpu.make_async_remote_copy(
            src_ref=src, dst_ref=dst, send_sem=ss, recv_sem=rs, device_id=to, device_id_type=MESH
        )
        cp.start()
        pending.append(cp)
        return cp

    def rows(start, size):
        return pl.ds(pl.multiple_of(start, 16), size)

    def cols(h):
        return slice(h * DH, (h + 1) * DH)

    barrier = pltpu.get_barrier_semaphore()
    partners = [ypart(o) for o in yoffs] + [zpart(o) for o in zoffs]
    partners += [xpart(o) for o in xoffs] + [cpart]
    for to in partners:
        pl.semaphore_signal(barrier, inc=1, device_id=to, device_id_type=MESH)
    e_copy = pltpu.make_async_copy(e_hbm, e_v, esem)
    e_copy.start()

    for i in range(5):
        qf[2 * i:2 * i + 2] = q_ref[i].astype(F32)
        sf[2 * i:2 * i + 2] = sc_ref[i]
    deq = [qf[:SLOTS, i * 128:(i + 1) * 128] * sf[:SLOTS, i:i + 1] for i in range(D // 128)]
    sq = sum(d * d for d in deq)
    inv = lax.rsqrt(jnp.sum(sq, axis=1, keepdims=True) * (1.0 / D) + 1e-6)
    xcat[...] = jnp.zeros_like(xcat)
    for i in range(D // 128):
        h, rest = divmod(i * 128, DH)
        cc, lane = divmod(rest, CW)
        gn = gain_ref[:, i * 128:(i + 1) * 128]
        xcat[h, cc * SP:cc * SP + SLOTS, lane:lane + 128] = (deq[i] * inv * gn).astype(BF16)

    def bar_len(seq, row):
        n = jnp.zeros(seq.shape, jnp.int32)
        for s in range(8):
            n = jnp.where(seq == s, cnt_ref[s], n)
        return jnp.clip(n - 64 * row, 0, 64)

    def bar_axis(dim):
        b = iota((1, 128) if dim == 1 else (BARS, 1), dim)
        return b, jnp.where(b < BARS, bar_len(jnp.bitwise_and(b, 7), lax.shift_right_logical(b, 3)), 0)

    def rank_of(seq, row, dim):
        b, lb = bar_axis(dim)
        mine, ml = row * 8 + seq, bar_len(seq, row)
        return count((lb > ml) | ((lb == ml) & (b < mine)), dim), ml

    def depth(kk, dim):
        _, lb = bar_axis(dim)
        return lax.shift_right_logical(jnp.maximum(lb - kk, 0) + 7, 3)

    def ahead(zz, nz, dim):
        return jnp.sum(jnp.minimum(zz, nz).astype(F32), axis=dim, keepdims=True).astype(jnp.int32)

    def slot_code(i, dim):
        seq, row = y * 2 + jnp.bitwise_and(i, 1), lax.shift_right_logical(i, 1)
        rank, ml = rank_of(seq, row, dim)
        before = ahead(jnp.full(i.shape, z, jnp.int32), depth(k, dim), dim)
        code = jnp.bitwise_and(rank + before, 3) * 8 + lax.shift_right_logical(rank, 2)
        return jnp.where((v < ml) & (i < SLOTS), code, -1)

    shape = (NY * ROWS, NK * SP)
    i0 = iota((NY * ROWS, 1), 0)
    o_i = div48(i0)
    ci = div6(i0 - o_i * ROWS)
    ri = i0 - o_i * ROWS - ci * CAPR
    want = jnp.bitwise_and(y + o_i, NY - 1) * 8 + ri
    j0 = iota((1, NK * SP), 1)
    cj = lax.shift_right_logical(j0, 4)
    code_j = slot_code(jnp.bitwise_and(j0, SP - 1), 0)
    pick = onehot(
        (jnp.broadcast_to(ci, shape) == jnp.broadcast_to(cj, shape))
        & (jnp.broadcast_to(want, shape) == jnp.broadcast_to(code_j, shape))
    )
    for h in range(H):
        blocks = jnp.dot(pick, xcat[h], preferred_element_type=F32).astype(BF16)
        for o in range(NY):
            sb[o, h] = blocks[o * ROWS:(o + 1) * ROWS]

    pl.semaphore_wait(barrier, len(partners))

    ycp = {}
    for a, b in Y_OUT:
        for o in yoffs:
            src, dst = sb.at[o, a:b], yr.at[o, a:b]
            ycp[a, o] = send(src, dst, ysend.at[a, o], yrecv.at[a, o], ypart(o))

    def place(i, dim):
        zz = div48(i)
        cc = div6(i - zz * ROWS)
        rr = i - zz * ROWS - cc * CAPR
        nz = depth(k, dim)
        before = ahead(zz, nz, dim)
        live = count(nz > zz, dim)
        rank = 4 * rr + jnp.bitwise_and(y - before, 3)
        p = lax.shift_right_logical(before + rank, 2)
        at = jnp.where(p < LR, cc * LR + p, MAIN + cc * OVR + p - LR)
        return jnp.where(rank < live, at, -1)

    perm1[...] = onehot(jnp.broadcast_to(place(iota((1, GR), 1), 0), (M, GR)) == iota((M, GR), 0))

    zcp = {}
    for h in range(H):
        for o in yoffs:
            if (h, o) in ycp:
                ycp[h, o].wait_recv()
        own = sb[0, h].astype(F32)
        for o in yoffs:
            own = own + yr[o, h].astype(F32)
        g[h, rows(z * ROWS, ROWS), :] = own.astype(BF16)
        for a, b in Z_OUT:
            if b == h + 1:
                mine = g.at[a:b, rows(z * ROWS, ROWS)]
                for o in zoffs:
                    zcp[a, o] = send(mine, mine, zsend.at[a, o], zrecv.at[a, o], zpart(o))

    si = iota((128, 1), 0)
    sa, sbb = lax.shift_right_logical(si, 4), jnp.bitwise_and(lax.shift_right_logical(si, 1), 7)
    swap[...] = onehot(
        jnp.broadcast_to(sbb * 16 + sa * 2 + jnp.bitwise_and(si, 1), (128, 128)) == iota((128, 128), 1)
    )
    perm2[...] = onehot(
        jnp.broadcast_to(place(iota((GR, 1), 0), 1), (GR, M)) == iota((GR, M), 1)
    )
    shape = (NK * SP, NY * ROWS)
    j0 = iota((1, NY * ROWS), 1)
    o_j = div48(j0)
    cj = div6(j0 - o_j * ROWS)
    rj = j0 - o_j * ROWS - cj * CAPR
    have = jnp.bitwise_and(y + NY - o_j, NY - 1) * 8 + rj
    i0 = iota((NK * SP, 1), 0)
    ci = lax.shift_right_logical(i0, 4)
    code_i = slot_code(jnp.bitwise_and(i0, SP - 1), 1)
    back[...] = onehot(
        (jnp.broadcast_to(ci, shape) == jnp.broadcast_to(cj, shape))
        & (jnp.broadcast_to(code_i, shape) == jnp.broadcast_to(have, shape))
    )

    xcp, ccp = {}, {}
    for h in range(H):
        for o in zoffs:
            if (h, o) in zcp:
                zcp[h, o].wait_recv()
        lg[h, line] = jnp.dot(perm1[...], g[h], preferred_element_type=F32).astype(BF16)
        mine = lg.at[h, line]
        for o in xoffs:
            xcp[h, o] = send(mine, mine, xsend.at[h, o], xrecv.at[h, o], xpart(o))

    def mm1(h):
        ccp[h].wait_recv()
        for ln in range(NK):
            for cc in range(NK):
                at = slice(h * DH + cc * CW, h * DH + (cc + 1) * CW)
                x_v[ln * LR:(ln + 1) * LR, at] = lg[h, ln, cc * LR:(cc + 1) * LR]
        stack = jnp.concatenate([lg[h, ln, MAIN:] for ln in range(NK)], axis=0)
        further = jnp.dot(swap[...], stack, preferred_element_type=F32).astype(BF16)
        for cc in range(NK):
            x_v[MAIN:, h * DH + cc * CW:h * DH + (cc + 1) * CW] = further[cc * OV:(cc + 1) * OV]
        if h == 0:
            e_copy.wait()

        def body(i, carry):
            n = pl.ds(pl.multiple_of(i * 640, 640), 640)
            part = lax.dot_general(
                x_v[:, cols(h)], e_v[n, cols(h)],
                (((1,), (1,)), ((), ())), preferred_element_type=F32,
            )
            l_v[:, n] = part if h == 0 else l_v[:, n] + part
            return carry

        lax.fori_loop(0, V // 640, body, 0)

    for h in range(H):
        for o in (1, 3, 2):
            xcp[h, o].wait_recv()
        mine = lg.at[h, pl.ds(c * NX, NX)]
        ccp[h] = send(mine, mine, csend.at[h], crecv.at[h], cpart)
        if h:
            mm1(h - 1)
    mm1(H - 1)

    for start, size in ((0, 128), (128, 128), (MAIN, OV)):
        r = slice(start, start + size)
        t1 = l_v[r, 0:128]
        t2 = jnp.full((size, 128), -jnp.inf, F32)
        for j in range(1, V // 128):
            val = l_v[r, j * 128:(j + 1) * 128]
            t2 = jnp.maximum(t2, jnp.minimum(t1, val))
            t1 = jnp.maximum(t1, val)
        top = jnp.max(t1, axis=1, keepdims=True)
        acc = jnp.zeros((size, 128), F32)
        for j in range(V // 128):
            e = jnp.exp(l_v[r, j * 128:(j + 1) * 128] - top)
            acc = acc + e
            p_v[r, j * 128:(j + 1) * 128] = e.astype(BF16)
        if size < 128:
            pad = jnp.ones((128 - size, 128), F32)
            t1, t2, acc = (jnp.concatenate([a, pad], axis=0) for a in (t1, t2, acc))
        for n, a in enumerate((t1, t2, acc)):
            tt[n, :, start:start + 128] = a.T
    m1, m2, sm = tt[0], tt[1], tt[2]
    n = 128
    while n > 1:
        n //= 2
        a1, b1 = m1[:n], m1[n:]
        m2 = jnp.maximum(jnp.minimum(a1, b1), jnp.maximum(m2[:n], m2[n:]))
        m1 = jnp.maximum(a1, b1)
        sm = sm[:n] + sm[n:]
    loc = m1

    def put(slot, parts):
        for n in range(3):
            st_o[slot, n:n + 1] = parts[n]

    def got3(ref):
        return (ref[0:1], ref[1:2], ref[2:3])

    def spread(ref, factor):
        for i in range(0, ML, 128):
            size = min(128, M - i)
            ref[i:i + size] = jnp.broadcast_to(factor[:, i:i + 128], (128, 128)).T[:size]

    c2, x2, z2, y2 = {}, {}, {}, {}

    def mm2(h):
        obf[:, cols(h)] = jnp.dot(p_v[...], e_v[:, cols(h)], preferred_element_type=F32).astype(BF16)

    def core_send(h):
        src = obf.at[rows((1 - c) * NX * LR, NX * LR), pl.ds(h * DH, DH)]
        c2[h, 0] = send(src, cr.at[h], c2send.at[h, 0], c2recv.at[h, 0], cpart)
        stack = jnp.concatenate(
            [obf[MAIN:, h * DH + cc * CW:h * DH + (cc + 1) * CW] for cc in range(NK)], axis=0
        )
        ovo[h] = jnp.dot(swap[...], stack, preferred_element_type=F32).astype(BF16)
        src = ovo.at[h, rows((1 - c) * NX * OV, NX * OV)]
        c2[h, 1] = send(src, cro.at[h], c2send.at[h, 1], c2recv.at[h, 1], cpart)

    st_o[...] = jnp.zeros_like(st_o)
    cur = (m1, m2, sm)
    put(0, cur)
    cp = send(st_o.at[0], st_c, scs, scr, cpart)
    mm2(0)
    core_send(0)
    cp.wait_recv()
    loc2 = st_c[0:1]
    cur = merge([cur, got3(st_c)])
    chip = cur[0]
    put(1, cur)
    xst = [send(st_o.at[1], st_x.at[o], sxs.at[o], sxr.at[o], xpart(o)) for o in xoffs]
    spread(fsc, jnp.exp(loc - chip))
    spread(fs2, jnp.exp(loc2 - chip))

    def x2_send(h, o, to):
        x2[h, o] = send(xs.at[h, o], xr.at[h, o], x2send.at[h, o], x2recv.at[h, o], xpart(to))

    def further_factor(ref, ln):
        pair = [ref[pl.ds(MAIN + ln * OVR + e, 1)] for e in range(OVR)]
        return jnp.where(jnp.bitwise_and(iota((OV, 128), 0), 1) == 0, pair[0], pair[1])

    def chip_sum(h, o):
        xx = xo(o)
        ln = c * NX + xx
        at = rows(ln * LR, LR)
        fa, fb = fsc[at], fs2[at]
        for lane in range(0, DH, 128):
            mine = obf[at, h * DH + lane:h * DH + lane + 128].astype(F32)
            theirs = cr[h, rows(xx * LR, LR), lane:lane + 128].astype(F32)
            cc, sub = divmod(lane, CW)
            xs[h, o, cc * LR:(cc + 1) * LR, sub:sub + 128] = (mine * fa + theirs * fb).astype(BF16)
        fa, fb = further_factor(fsc, ln), further_factor(fs2, ln)
        for sub in range(0, CW, 128):
            mine = ovo[h, rows(ln * OV, OV), sub:sub + 128].astype(F32)
            theirs = cro[h, rows(xx * OV, OV), sub:sub + 128].astype(F32)
            xs[h, o, MAIN:, sub:sub + 128] = (mine * fa + theirs * fb).astype(BF16)

    def chip_sums(h):
        c2[h, 0].wait_recv()
        c2[h, 1].wait_recv()
        for o in (2, 1, 3, 0):
            chip_sum(h, o)
            if o:
                x2_send(h, o, o)

    for h in range(1, H):
        mm2(h)
        core_send(h)
        chip_sums(h - 1)
    chip_sums(H - 1)

    for cp in xst:
        cp.wait_recv()
    cur = merge([cur] + [got3(st_x[o]) for o in xoffs])
    put(2, cur)
    zst = [send(st_o.at[2], st_z.at[o], szs.at[o], szr.at[o], zpart(o)) for o in zoffs]
    for cp in zst:
        cp.wait_recv()
    m1, m2, sm = merge([cur] + [got3(st_z[o]) for o in zoffs])
    for o in range(NX):
        spread(fx.at[o], jnp.exp((st_x[o, 0:1] if o else chip) - m1) / sm * 64.0)
    margin = (1.0 - jnp.exp(m2 - m1)) / sm
    mg[y] = jnp.broadcast_to(margin, (8, ML))
    mcp = [send(mg.at[y], mg.at[y], ms.at[o], mr.at[o], ypart(o)) for o in yoffs]

    f_main = [fx[o, rows(line * LR, LR)] for o in range(NX)]
    f_ov = [further_factor(fx.at[o], line) for o in range(NX)]

    for h in range(H):
        for o in (1, 3, 2):
            x2[h, o].wait_recv()
        for lane in range(0, CW, 128):
            ln = slice(lane, lane + 128)
            for cc in range(NK + 1):
                r = slice(cc * LR, min(cc * LR + LR, M))
                f = f_main if cc < NK else f_ov
                tot = xs[h, 0, r, ln].astype(F32) * f[0]
                for o in xoffs:
                    tot = tot + xr[h, o, r, ln].astype(F32) * f[o]
                pst[r, ln] = tot.astype(BF16)
        zs[h] = jnp.dot(perm2[...], pst[...], preferred_element_type=F32).astype(BF16)
        for a, b in Z_BACK:
            if b == h + 1:
                for o in zoffs:
                    src = zs.at[a:b, rows(lax.rem(z + o, NZ) * ROWS, ROWS)]
                    dst = zr.at[o, a:b]
                    z2[a, o] = send(src, dst, z2send.at[a, o], z2recv.at[a, o], zpart(o))

    for cp in mcp:
        cp.wait_recv()
    lane = iota((1, ML), 1)
    lm = jnp.minimum(lane, M - 1)
    ln = jnp.where(lm < MAIN, lax.shift_right_logical(lm, 5), lax.shift_right_logical(lm - MAIN, 1))
    p = jnp.where(lm < MAIN, jnp.bitwise_and(lm, LR - 1), LR + jnp.bitwise_and(lm, 1))
    kk = jnp.bitwise_and(ln, NX - 1) * NC + lax.shift_right_logical(ln, 2)
    nz = depth(kk, 0)
    befores = [ahead(jnp.full((1, ML), n, jnp.int32), nz, 0) for n in range(NZ + 1)]
    slot = iota((SP, 1), 0)
    rank_i, len_i = rank_of(y * 2 + jnp.bitwise_and(slot, 1), lax.shift_right_logical(slot, 1), 1)
    by_col = jnp.zeros((SP, 64), F32)
    for yy in range(NY):
        gi = 4 * p + yy
        zz = jnp.zeros((1, ML), jnp.int32)
        first = jnp.zeros((1, ML), jnp.int32)
        for n in range(1, NZ):
            past = befores[n] <= gi
            zz = jnp.where(past, n, zz)
            first = jnp.where(past, befores[n], first)
        rank = jnp.where((gi < befores[NZ]) & (lane < M), gi - first, -1)
        vals = jnp.where(
            jnp.broadcast_to(rank, (SP, ML)) == jnp.broadcast_to(rank_i, (SP, ML)),
            jnp.broadcast_to(mg[yy, 0:1], (SP, ML)), 0.0,
        )
        hit = jnp.broadcast_to(zz * NK + kk, (64, ML)) == iota((64, ML), 0)
        by_col = by_col + lax.dot_general(
            vals, jnp.where(hit, 1.0, 0.0), (((1,), (1,)), ((), ())),
            preferred_element_type=F32, precision=lax.Precision.HIGHEST,
        )
    masked = (iota((SP, 64), 1) < len_i) & (iota((SP, 64), 0) < SLOTS)
    by_col = jnp.where(masked, by_col, 0.0)
    wide = (2, 128)
    marg = jnp.zeros(wide, F32)
    for t in range(LEN_DEV):
        target = v * LEN_DEV + t
        for s2 in range(2):
            hit = sum(
                jnp.where(pos_ref[r5, s2:s2 + 1] == target, by_col[2 * r5 + s2:2 * r5 + s2 + 1], 0.0)
                for r5 in range(5)
            )
            val = jnp.broadcast_to(jnp.sum(hit, axis=1, keepdims=True), wide)
            marg = jnp.where((iota(wide, 1) == t) & (iota(wide, 0) == s2), val, marg)
    marg_ref[...] = marg[:, :LEN_DEV]

    for h in range(H):
        for o in zoffs:
            if (h, o) in z2:
                z2[h, o].wait_recv()
        tot = zs[h, rows(z * ROWS, ROWS), :].astype(F32)
        for o in zoffs:
            tot = tot + zr[o, h].astype(F32)
        yr2[0, h] = tot.astype(BF16)
        for a, b in Y_BACK:
            if b == h + 1:
                for o in yoffs:
                    src, dst = yr2.at[0, a:b], yr2.at[o, a:b]
                    y2[a, o] = send(src, dst, y2send.at[a, o], y2recv.at[a, o], ypart(o))

    for h in range(H):
        for o in yoffs:
            if (h, o) in y2:
                y2[h, o].wait_recv()
        cat = jnp.concatenate([yr2[o, h] for o in range(NY)], axis=0)
        got = jnp.dot(back[...], cat, preferred_element_type=F32)
        for cc in range(NK):
            res[:, h * DH + cc * CW:h * DH + (cc + 1) * CW] = got[cc * SP:(cc + 1) * SP]
    for i in range(5):
        out_ref[i] = res[2 * i:2 * i + 2].astype(BF16)
    for cp in pending:
        cp.wait_send()


def readout(q, sc, gain, table, counts, positions):
    dma = pltpu.SemaphoreType.DMA
    vm = pl.BlockSpec(memory_space=pltpu.VMEM)
    return pl.pallas_call(
        kernel,
        out_shape=(
            jax.ShapeDtypeStruct(q.shape, BF16),
            jax.ShapeDtypeStruct((2, LEN_DEV), F32),
        ),
        in_specs=[
            vm, vm, vm, pl.BlockSpec(memory_space=pl.ANY), pl.BlockSpec(memory_space=pltpu.SMEM), vm
        ],
        out_specs=(vm, vm),
        scratch_shapes=[
            pltpu.VMEM((V, D), BF16),
            pltpu.VMEM((SP, D), F32),
            pltpu.VMEM((SP, D // 128), F32),
            pltpu.VMEM((H, NK * SP, CW), BF16),
            pltpu.VMEM((NY, H, ROWS, CW), BF16),
            pltpu.VMEM((NY, H, ROWS, CW), BF16),
            pltpu.VMEM((H, GR, CW), BF16),
            pltpu.VMEM((M, GR), BF16),
            pltpu.VMEM((GR, M), BF16),
            pltpu.VMEM((128, 128), BF16),
            pltpu.VMEM((NK * SP, NY * ROWS), BF16),
            pltpu.VMEM((M, D), BF16),
            pltpu.VMEM((H, NK, M, CW), BF16),
            pltpu.VMEM((M, V), F32),
            pltpu.VMEM((M, V), BF16),
            pltpu.VMEM((3, 128, ML), F32),
            pltpu.VMEM((M, 128), F32),
            pltpu.VMEM((M, 128), F32),
            pltpu.VMEM((NX, M, 128), F32),
            pltpu.VMEM((M, D), BF16),
            pltpu.VMEM((H, NK * OV, CW), BF16),
            pltpu.VMEM((H, NX * LR, DH), BF16),
            pltpu.VMEM((H, NX * OV, CW), BF16),
            pltpu.VMEM((H, NX, M, CW), BF16),
            pltpu.VMEM((H, NX, M, CW), BF16),
            pltpu.VMEM((M, CW), BF16),
            pltpu.VMEM((H, GR, CW), BF16),
            pltpu.VMEM((NZ, H, ROWS, CW), BF16),
            pltpu.VMEM((NY, H, ROWS, CW), BF16),
            pltpu.VMEM((SP, D), F32),
            pltpu.VMEM((NY, 8, ML), F32),
            pltpu.VMEM((8, ML), F32),
            pltpu.VMEM((NX, 8, ML), F32),
            pltpu.VMEM((NZ, 8, ML), F32),
            pltpu.VMEM((3, 8, ML), F32),
            dma,
            dma((H, NY)), dma((H, NY)), dma((H, NZ)), dma((H, NZ)),
            dma((H, NX)), dma((H, NX)), dma((H,)), dma((H,)),
            dma((H, 2)), dma((H, 2)), dma((H, NX)), dma((H, NX)),
            dma((H, NZ)), dma((H, NZ)), dma((H, NY)), dma((H, NY)),
            dma, dma, dma((NX,)), dma((NX,)), dma((NZ,)), dma((NZ,)), dma((NY,)), dma((NY,)),
        ],
        compiler_params=pltpu.CompilerParams(
            collective_id=0, has_side_effects=True, vmem_limit_bytes=60 << 20
        ),
        cost_estimate=pl.CostEstimate(
            flops=4 * M * V * D, bytes_accessed=2 * V * D, transcendentals=M * V
        ),
        name="readout",
    )(q, sc, gain, table, counts, positions)


def hand_out(a, b, out_a, out_b):
    out_a[...] = a[...]
    out_b[...] = b[...]


def on_device(quantized, scales, norm_gain, embed_table, counts, positions):
    expected, margins = readout(
        quantized[0], scales[0], norm_gain.reshape(1, D), embed_table, counts,
        positions.transpose(1, 2, 0),
    )
    vm = pl.BlockSpec(memory_space=pltpu.VMEM)
    expected, margins = pl.pallas_call(
        hand_out,
        out_shape=tuple(jax.ShapeDtypeStruct(a.shape, a.dtype) for a in (expected, margins)),
        in_specs=[vm, vm], out_specs=(vm, vm), name="hand_out",
    )(expected, margins)
    return (expected[None], margins)


def solution(mesh):
    in_specs = (
        P("vocab", None, "pos", None),
        P("vocab", None, "pos", None),
        P(),
        P("vocab", None),
        P(),
        P(None, None, "pos"),
    )
    out_specs = (P("vocab", None, "pos", None), P("pos", "vocab"))
    return jax.shard_map(
        on_device, mesh=mesh, in_specs=in_specs, out_specs=out_specs, check_vma=False
    )
```

```python
import functools

import jax
import jax.numpy as jnp
from jax import lax
from jax.experimental import pallas as pl
from jax.experimental.pallas import tpu as pltpu
from jax.sharding import PartitionSpec as P

MESH = pl.DeviceIdType.MESH
F32 = jnp.float32
BF16 = jnp.bfloat16

D = 4096
LEN_DEV = 10
NY, NZ, NX, NC = 4, 8, 4, 2
NK = NX * NC
CAPR = 6
ROWS = NK * CAPR
GR = NZ * ROWS
LR = 32
OVR = 2
MAIN = NK * LR
OV = NK * OVR
M = MAIN + OV
ML = 384
V = 1280
H = 4
DH = D // H
CW = DH // NK
SLOTS = 10
SP = 16
BARS = 40
Y_OUT = ((0, 1), (1, 2), (2, 3), (3, 4))
Z_OUT = ((0, 1), (1, 2), (2, 3), (3, 4))
Z_BACK = ((0, 1), (1, 2), (2, 3), (3, 4))
Y_BACK = ((0, 1), (1, 2), (2, 3), (3, 4))


def onehot(cond):
    return jnp.where(cond, 1.0, 0.0).astype(BF16)


def iota(shape, dim):
    return lax.broadcasted_iota(jnp.int32, shape, dim)


def div48(i):
    return lax.shift_right_logical(i * 683, 15)


def div6(i):
    return lax.shift_right_logical(i * 43, 8)


def count(cond, axis):
    return jnp.sum(jnp.where(cond, 1.0, 0.0), axis=axis, keepdims=True).astype(jnp.int32)


def merge(parts):
    top = functools.reduce(jnp.maximum, [p[0] for p in parts])
    total = sum(p[2] * jnp.exp(p[0] - top) for p in parts)
    m1, m2 = parts[0][0], parts[0][1]
    for p in parts[1:]:
        m2 = jnp.maximum(jnp.minimum(m1, p[0]), jnp.maximum(m2, p[1]))
        m1 = jnp.maximum(m1, p[0])
    return m1, m2, total


def kernel(
    q_ref, sc_ref, gain_ref, e_hbm, cnt_ref, pos_ref,
    out_ref, marg_ref,
    e_v, qf, sf, xcat, sb, yr, g, perm1, perm2, swap, back, x_v, lg, l_v, p_v, tt, fsc, fs2, fx, obf,
    ovo, cr, cro, xs, xr, pst, zs, zr, yr2, res, mg, st_c, st_x, st_z, st_o,
    esem, ysend, yrecv, zsend, zrecv, xsend, xrecv, csend, crecv,
    c2send, c2recv, x2send, x2recv, z2send, z2recv, y2send, y2recv,
    scs, scr, sxs, sxr, szs, szr, ms, mr,
):
    y = lax.axis_index("pos")
    v = lax.axis_index("vocab")
    z = v // NK
    k = lax.rem(v, NK)
    x = k // NC
    c = lax.rem(k, NC)
    line = c * NX + x

    def dev(yy, zz, xx, cc):
        return (yy, zz * NK + xx * NC + cc)

    def xo(o):
        return lax.rem(x + o, NX)

    def ypart(o):
        return dev(lax.rem(y + o, NY), z, x, c)

    def zpart(o):
        return dev(y, lax.rem(z + o, NZ), x, c)

    def xpart(o):
        return dev(y, z, xo(o), c)

    cpart = dev(y, z, x, 1 - c)
    yoffs, zoffs, xoffs = (1, 3, 2), (4, 3, 5, 2, 6, 1, 7), (2, 1, 3)
    pending = []

    def send(src, dst, ss, rs, to):
        cp = pltpu.make_async_remote_copy(
            src_ref=src, dst_ref=dst, send_sem=ss, recv_sem=rs, device_id=to, device_id_type=MESH
        )
        cp.start()
        pending.append(cp)
        return cp

    def drain(keep=()):
        kept = [cp for cp in pending if any(cp is k for k in keep)]
        for cp in pending:
            if not any(cp is k for k in keep):
                cp.wait_send()
        pending[:] = kept

    def rows(start, size):
        return pl.ds(pl.multiple_of(start, 16), size)

    def cols(h):
        return slice(h * DH, (h + 1) * DH)

    barrier = pltpu.get_barrier_semaphore()
    partners = [ypart(o) for o in yoffs] + [zpart(o) for o in zoffs]
    partners += [xpart(o) for o in xoffs] + [cpart]
    for to in partners:
        pl.semaphore_signal(barrier, inc=1, device_id=to, device_id_type=MESH)
    e_copy = pltpu.make_async_copy(e_hbm, e_v, esem)
    e_copy.start()

    for i in range(5):
        qf[2 * i:2 * i + 2] = q_ref[i].astype(F32)
        sf[2 * i:2 * i + 2] = sc_ref[i]
    deq = [qf[:SLOTS, i * 128:(i + 1) * 128] * sf[:SLOTS, i:i + 1] for i in range(D // 128)]
    sq = sum(d * d for d in deq)
    inv = lax.rsqrt(jnp.sum(sq, axis=1, keepdims=True) * (1.0 / D) + 1e-6)
    xcat[...] = jnp.zeros_like(xcat)
    for i in range(D // 128):
        h, rest = divmod(i * 128, DH)
        cc, lane = divmod(rest, CW)
        gn = gain_ref[:, i * 128:(i + 1) * 128]
        xcat[h, cc * SP:cc * SP + SLOTS, lane:lane + 128] = (deq[i] * inv * gn).astype(BF16)

    def bar_len(seq, row):
        n = jnp.zeros(seq.shape, jnp.int32)
        for s in range(8):
            n = jnp.where(seq == s, cnt_ref[s], n)
        return jnp.clip(n - 64 * row, 0, 64)

    def bar_axis(dim):
        b = iota((1, 128) if dim == 1 else (BARS, 1), dim)
        return b, jnp.where(b < BARS, bar_len(jnp.bitwise_and(b, 7), lax.shift_right_logical(b, 3)), 0)

    def rank_of(seq, row, dim):
        b, lb = bar_axis(dim)
        mine, ml = row * 8 + seq, bar_len(seq, row)
        return count((lb > ml) | ((lb == ml) & (b < mine)), dim), ml

    def depth(kk, dim):
        _, lb = bar_axis(dim)
        return lax.shift_right_logical(jnp.maximum(lb - kk, 0) + 7, 3)

    def ahead(zz, nz, dim):
        return jnp.sum(jnp.minimum(zz, nz).astype(F32), axis=dim, keepdims=True).astype(jnp.int32)

    def slot_code(i, dim):
        seq, row = y * 2 + jnp.bitwise_and(i, 1), lax.shift_right_logical(i, 1)
        rank, ml = rank_of(seq, row, dim)
        before = ahead(jnp.full(i.shape, z, jnp.int32), depth(k, dim), dim)
        code = jnp.bitwise_and(rank + before, 3) * 8 + lax.shift_right_logical(rank, 2)
        return jnp.where((v < ml) & (i < SLOTS), code, -1)

    shape = (NY * ROWS, NK * SP)
    i0 = iota((NY * ROWS, 1), 0)
    o_i = div48(i0)
    ci = div6(i0 - o_i * ROWS)
    ri = i0 - o_i * ROWS - ci * CAPR
    want = jnp.bitwise_and(y + o_i, NY - 1) * 8 + ri
    j0 = iota((1, NK * SP), 1)
    cj = lax.shift_right_logical(j0, 4)
    code_j = slot_code(jnp.bitwise_and(j0, SP - 1), 0)
    pick = onehot(
        (jnp.broadcast_to(ci, shape) == jnp.broadcast_to(cj, shape))
        & (jnp.broadcast_to(want, shape) == jnp.broadcast_to(code_j, shape))
    )
    for h in range(H):
        blocks = jnp.dot(pick, xcat[h], preferred_element_type=F32).astype(BF16)
        for o in range(NY):
            sb[o, h] = blocks[o * ROWS:(o + 1) * ROWS]

    pl.semaphore_wait(barrier, len(partners))

    ycp = {}
    for a, b in Y_OUT:
        for o in yoffs:
            src, dst = sb.at[o, a:b], yr.at[o, a:b]
            ycp[a, o] = send(src, dst, ysend.at[a, o], yrecv.at[a, o], ypart(o))

    def place(i, dim):
        zz = div48(i)
        cc = div6(i - zz * ROWS)
        rr = i - zz * ROWS - cc * CAPR
        nz = depth(k, dim)
        before = ahead(zz, nz, dim)
        live = count(nz > zz, dim)
        rank = 4 * rr + jnp.bitwise_and(y - before, 3)
        p = lax.shift_right_logical(before + rank, 2)
        at = jnp.where(p < LR, cc * LR + p, MAIN + cc * OVR + p - LR)
        return jnp.where(rank < live, at, -1)

    perm1[...] = onehot(jnp.broadcast_to(place(iota((1, GR), 1), 0), (M, GR)) == iota((M, GR), 0))

    zcp = {}
    for h in range(H):
        for o in yoffs:
            if (h, o) in ycp:
                ycp[h, o].wait_recv()
        own = sb[0, h].astype(F32)
        for o in yoffs:
            own = own + yr[o, h].astype(F32)
        g[h, rows(z * ROWS, ROWS), :] = own.astype(BF16)
        for a, b in Z_OUT:
            if b == h + 1:
                mine = g.at[a:b, rows(z * ROWS, ROWS)]
                for o in zoffs:
                    zcp[a, o] = send(mine, mine, zsend.at[a, o], zrecv.at[a, o], zpart(o))

    si = iota((128, 1), 0)
    sa, sbb = lax.shift_right_logical(si, 4), jnp.bitwise_and(lax.shift_right_logical(si, 1), 7)
    swap[...] = onehot(
        jnp.broadcast_to(sbb * 16 + sa * 2 + jnp.bitwise_and(si, 1), (128, 128)) == iota((128, 128), 1)
    )
    perm2[...] = onehot(
        jnp.broadcast_to(place(iota((GR, 1), 0), 1), (GR, M)) == iota((GR, M), 1)
    )
    shape = (NK * SP, NY * ROWS)
    j0 = iota((1, NY * ROWS), 1)
    o_j = div48(j0)
    cj = div6(j0 - o_j * ROWS)
    rj = j0 - o_j * ROWS - cj * CAPR
    have = jnp.bitwise_and(y + NY - o_j, NY - 1) * 8 + rj
    i0 = iota((NK * SP, 1), 0)
    ci = lax.shift_right_logical(i0, 4)
    code_i = slot_code(jnp.bitwise_and(i0, SP - 1), 1)
    back[...] = onehot(
        (jnp.broadcast_to(ci, shape) == jnp.broadcast_to(cj, shape))
        & (jnp.broadcast_to(code_i, shape) == jnp.broadcast_to(have, shape))
    )

    xcp, ccp = {}, {}
    for h in range(H):
        for o in zoffs:
            if (h, o) in zcp:
                zcp[h, o].wait_recv()
        lg[h, line] = jnp.dot(perm1[...], g[h], preferred_element_type=F32).astype(BF16)
        mine = lg.at[h, line]
        for o in xoffs:
            xcp[h, o] = send(mine, mine, xsend.at[h, o], xrecv.at[h, o], xpart(o))

    def mm1(h):
        ccp[h].wait_recv()
        for ln in range(NK):
            for cc in range(NK):
                at = slice(h * DH + cc * CW, h * DH + (cc + 1) * CW)
                x_v[ln * LR:(ln + 1) * LR, at] = lg[h, ln, cc * LR:(cc + 1) * LR]
        stack = jnp.concatenate([lg[h, ln, MAIN:] for ln in range(NK)], axis=0)
        further = jnp.dot(swap[...], stack, preferred_element_type=F32).astype(BF16)
        for cc in range(NK):
            x_v[MAIN:, h * DH + cc * CW:h * DH + (cc + 1) * CW] = further[cc * OV:(cc + 1) * OV]
        if h == 0:
            e_copy.wait()

        part = lax.dot_general(
            x_v[:, cols(h)], e_v[:, cols(h)],
            (((1,), (1,)), ((), ())), preferred_element_type=F32,
        )
        l_v[...] = part if h == 0 else l_v[...] + part

    for h in range(H):
        for o in (1, 3, 2):
            xcp[h, o].wait_recv()
        mine = lg.at[h, pl.ds(c * NX, NX)]
        ccp[h] = send(mine, mine, csend.at[h], crecv.at[h], cpart)
        if h:
            mm1(h - 1)
    mm1(H - 1)

    for start, size in ((0, 128), (128, 128), (MAIN, OV)):
        r = slice(start, start + size)
        t1 = l_v[r, 0:128]
        t2 = jnp.full((size, 128), -jnp.inf, F32)
        for j in range(1, V // 128):
            val = l_v[r, j * 128:(j + 1) * 128]
            t2 = jnp.maximum(t2, jnp.minimum(t1, val))
            t1 = jnp.maximum(t1, val)
        top = jnp.max(t1, axis=1, keepdims=True)
        acc = jnp.zeros((size, 128), F32)
        for j in range(V // 128):
            e = jnp.exp(l_v[r, j * 128:(j + 1) * 128] - top)
            acc = acc + e
            p_v[r, j * 128:(j + 1) * 128] = e.astype(BF16)
        if size < 128:
            pad = jnp.ones((128 - size, 128), F32)
            t1, t2, acc = (jnp.concatenate([a, pad], axis=0) for a in (t1, t2, acc))
        for n, a in enumerate((t1, t2, acc)):
            tt[n, :, start:start + 128] = a.T
    m1, m2, sm = tt[0], tt[1], tt[2]
    n = 128
    while n > 1:
        n //= 2
        a1, b1 = m1[:n], m1[n:]
        m2 = jnp.maximum(jnp.minimum(a1, b1), jnp.maximum(m2[:n], m2[n:]))
        m1 = jnp.maximum(a1, b1)
        sm = sm[:n] + sm[n:]
    loc = m1

    def put(slot, parts):
        for n in range(3):
            st_o[slot, n:n + 1] = parts[n]

    def got3(ref):
        return (ref[0:1], ref[1:2], ref[2:3])

    def spread(ref, factor):
        for i in range(0, ML, 128):
            size = min(128, M - i)
            ref[i:i + size] = jnp.broadcast_to(factor[:, i:i + 128], (128, 128)).T[:size]

    c2, x2, z2, y2 = {}, {}, {}, {}

    def mm2(h):
        obf[:, cols(h)] = jnp.dot(p_v[...], e_v[:, cols(h)], preferred_element_type=F32).astype(BF16)

    def core_send(h):
        src = obf.at[rows((1 - c) * NX * LR, NX * LR), pl.ds(h * DH, DH)]
        c2[h, 0] = send(src, cr.at[h], c2send.at[h, 0], c2recv.at[h, 0], cpart)
        stack = jnp.concatenate(
            [obf[MAIN:, h * DH + cc * CW:h * DH + (cc + 1) * CW] for cc in range(NK)], axis=0
        )
        ovo[h] = jnp.dot(swap[...], stack, preferred_element_type=F32).astype(BF16)
        src = ovo.at[h, rows((1 - c) * NX * OV, NX * OV)]
        c2[h, 1] = send(src, cro.at[h], c2send.at[h, 1], c2recv.at[h, 1], cpart)

    st_o[...] = jnp.zeros_like(st_o)
    cur = (m1, m2, sm)
    put(0, cur)
    cp = send(st_o.at[0], st_c, scs, scr, cpart)
    mm2(0)
    core_send(0)
    cp.wait_recv()
    loc2 = st_c[0:1]
    cur = merge([cur, got3(st_c)])
    chip = cur[0]
    put(1, cur)
    xst = [send(st_o.at[1], st_x.at[o], sxs.at[o], sxr.at[o], xpart(o)) for o in xoffs]
    spread(fsc, jnp.exp(loc - chip))
    spread(fs2, jnp.exp(loc2 - chip))

    def x2_send(h, o, to):
        x2[h, o] = send(xs.at[h, o], xr.at[h, o], x2send.at[h, o], x2recv.at[h, o], xpart(to))

    def further_factor(ref, ln):
        pair = [ref[pl.ds(MAIN + ln * OVR + e, 1)] for e in range(OVR)]
        return jnp.where(jnp.bitwise_and(iota((OV, 128), 0), 1) == 0, pair[0], pair[1])

    def chip_sum(h, o):
        xx = xo(o)
        ln = c * NX + xx
        at = rows(ln * LR, LR)
        fa, fb = fsc[at], fs2[at]
        for lane in range(0, DH, 128):
            mine = obf[at, h * DH + lane:h * DH + lane + 128].astype(F32)
            theirs = cr[h, rows(xx * LR, LR), lane:lane + 128].astype(F32)
            cc, sub = divmod(lane, CW)
            xs[h, o, cc * LR:(cc + 1) * LR, sub:sub + 128] = (mine * fa + theirs * fb).astype(BF16)
        fa, fb = further_factor(fsc, ln), further_factor(fs2, ln)
        for sub in range(0, CW, 128):
            mine = ovo[h, rows(ln * OV, OV), sub:sub + 128].astype(F32)
            theirs = cro[h, rows(xx * OV, OV), sub:sub + 128].astype(F32)
            xs[h, o, MAIN:, sub:sub + 128] = (mine * fa + theirs * fb).astype(BF16)

    def chip_sums(h):
        c2[h, 0].wait_recv()
        c2[h, 1].wait_recv()
        for o in (2, 1, 3, 0):
            chip_sum(h, o)
            if o:
                x2_send(h, o, o)

    for h in range(1, H):
        mm2(h)
        core_send(h)
        chip_sums(h - 1)
    chip_sums(H - 1)

    for cp in xst:
        cp.wait_recv()
    cur = merge([cur] + [got3(st_x[o]) for o in xoffs])
    put(2, cur)
    zst = [send(st_o.at[2], st_z.at[o], szs.at[o], szr.at[o], zpart(o)) for o in zoffs]
    for cp in zst:
        cp.wait_recv()
    m1, m2, sm = merge([cur] + [got3(st_z[o]) for o in zoffs])
    for o in range(NX):
        spread(fx.at[o], jnp.exp((st_x[o, 0:1] if o else chip) - m1) / sm * 64.0)
    margin = (1.0 - jnp.exp(m2 - m1)) / sm
    mg[y] = jnp.broadcast_to(margin, (8, ML))
    mcp = [send(mg.at[y], mg.at[y], ms.at[o], mr.at[o], ypart(o)) for o in yoffs]

    drain(list(x2.values()) + mcp)
    f_main = [fx[o, rows(line * LR, LR)] for o in range(NX)]
    f_ov = [further_factor(fx.at[o], line) for o in range(NX)]

    for h in range(H):
        for o in (1, 3, 2):
            x2[h, o].wait_recv()
        for lane in range(0, CW, 128):
            ln = slice(lane, lane + 128)
            for cc in range(NK + 1):
                r = slice(cc * LR, min(cc * LR + LR, M))
                f = f_main if cc < NK else f_ov
                tot = xs[h, 0, r, ln].astype(F32) * f[0]
                for o in xoffs:
                    tot = tot + xr[h, o, r, ln].astype(F32) * f[o]
                pst[r, ln] = tot.astype(BF16)
        zs[h] = jnp.dot(perm2[...], pst[...], preferred_element_type=F32).astype(BF16)
        for a, b in Z_BACK:
            if b == h + 1:
                for o in zoffs:
                    src = zs.at[a:b, rows(lax.rem(z + o, NZ) * ROWS, ROWS)]
                    dst = zr.at[o, a:b]
                    z2[a, o] = send(src, dst, z2send.at[a, o], z2recv.at[a, o], zpart(o))

    drain(list(z2.values()) + mcp)
    for cp in mcp:
        cp.wait_recv()
    lane = iota((1, ML), 1)
    lm = jnp.minimum(lane, M - 1)
    ln = jnp.where(lm < MAIN, lax.shift_right_logical(lm, 5), lax.shift_right_logical(lm - MAIN, 1))
    p = jnp.where(lm < MAIN, jnp.bitwise_and(lm, LR - 1), LR + jnp.bitwise_and(lm, 1))
    kk = jnp.bitwise_and(ln, NX - 1) * NC + lax.shift_right_logical(ln, 2)
    nz = depth(kk, 0)
    befores = [ahead(jnp.full((1, ML), n, jnp.int32), nz, 0) for n in range(NZ + 1)]
    slot = iota((SP, 1), 0)
    rank_i, len_i = rank_of(y * 2 + jnp.bitwise_and(slot, 1), lax.shift_right_logical(slot, 1), 1)
    by_col = jnp.zeros((SP, 64), F32)
    for yy in range(NY):
        gi = 4 * p + yy
        zz = jnp.zeros((1, ML), jnp.int32)
        first = jnp.zeros((1, ML), jnp.int32)
        for n in range(1, NZ):
            past = befores[n] <= gi
            zz = jnp.where(past, n, zz)
            first = jnp.where(past, befores[n], first)
        rank = jnp.where((gi < befores[NZ]) & (lane < M), gi - first, -1)
        vals = jnp.where(
            jnp.broadcast_to(rank, (SP, ML)) == jnp.broadcast_to(rank_i, (SP, ML)),
            jnp.broadcast_to(mg[yy, 0:1], (SP, ML)), 0.0,
        )
        hit = jnp.broadcast_to(zz * NK + kk, (64, ML)) == iota((64, ML), 0)
        by_col = by_col + lax.dot_general(
            vals, jnp.where(hit, 1.0, 0.0), (((1,), (1,)), ((), ())),
            preferred_element_type=F32, precision=lax.Precision.HIGHEST,
        )
    masked = (iota((SP, 64), 1) < len_i) & (iota((SP, 64), 0) < SLOTS)
    by_col = jnp.where(masked, by_col, 0.0)
    wide = (2, 128)
    marg = jnp.zeros(wide, F32)
    for t in range(LEN_DEV):
        target = v * LEN_DEV + t
        for s2 in range(2):
            hit = sum(
                jnp.where(pos_ref[r5, s2:s2 + 1] == target, by_col[2 * r5 + s2:2 * r5 + s2 + 1], 0.0)
                for r5 in range(5)
            )
            val = jnp.broadcast_to(jnp.sum(hit, axis=1, keepdims=True), wide)
            marg = jnp.where((iota(wide, 1) == t) & (iota(wide, 0) == s2), val, marg)
    marg_ref[...] = marg[:, :LEN_DEV]

    for h in range(H):
        for o in zoffs:
            if (h, o) in z2:
                z2[h, o].wait_recv()
        tot = zs[h, rows(z * ROWS, ROWS), :].astype(F32)
        for o in zoffs:
            tot = tot + zr[o, h].astype(F32)
        yr2[0, h] = tot.astype(BF16)
        for a, b in Y_BACK:
            if b == h + 1:
                for o in yoffs:
                    src, dst = yr2.at[0, a:b], yr2.at[o, a:b]
                    y2[a, o] = send(src, dst, y2send.at[a, o], y2recv.at[a, o], ypart(o))

    drain(y2.values())
    for h in range(H):
        for o in yoffs:
            if (h, o) in y2:
                y2[h, o].wait_recv()
        cat = jnp.concatenate([yr2[o, h] for o in range(NY)], axis=0)
        got = jnp.dot(back[...], cat, preferred_element_type=F32)
        for cc in range(NK):
            res[:, h * DH + cc * CW:h * DH + (cc + 1) * CW] = got[cc * SP:(cc + 1) * SP]
    for i in range(5):
        out_ref[i] = res[2 * i:2 * i + 2].astype(BF16)
    drain()


def readout(q, sc, gain, table, counts, positions):
    dma = pltpu.SemaphoreType.DMA
    vm = pl.BlockSpec(memory_space=pltpu.VMEM)
    return pl.pallas_call(
        kernel,
        out_shape=(
            jax.ShapeDtypeStruct(q.shape, BF16),
            jax.ShapeDtypeStruct((2, LEN_DEV), F32),
        ),
        in_specs=[
            vm, vm, vm, pl.BlockSpec(memory_space=pl.ANY), pl.BlockSpec(memory_space=pltpu.SMEM), vm
        ],
        out_specs=(vm, vm),
        scratch_shapes=[
            pltpu.VMEM((V, D), BF16),
            pltpu.VMEM((SP, D), F32),
            pltpu.VMEM((SP, D // 128), F32),
            pltpu.VMEM((H, NK * SP, CW), BF16),
            pltpu.VMEM((NY, H, ROWS, CW), BF16),
            pltpu.VMEM((NY, H, ROWS, CW), BF16),
            pltpu.VMEM((H, GR, CW), BF16),
            pltpu.VMEM((M, GR), BF16),
            pltpu.VMEM((GR, M), BF16),
            pltpu.VMEM((128, 128), BF16),
            pltpu.VMEM((NK * SP, NY * ROWS), BF16),
            pltpu.VMEM((M, D), BF16),
            pltpu.VMEM((H, NK, M, CW), BF16),
            pltpu.VMEM((M, V), F32),
            pltpu.VMEM((M, V), BF16),
            pltpu.VMEM((3, 128, ML), F32),
            pltpu.VMEM((M, 128), F32),
            pltpu.VMEM((M, 128), F32),
            pltpu.VMEM((NX, M, 128), F32),
            pltpu.VMEM((M, D), BF16),
            pltpu.VMEM((H, NK * OV, CW), BF16),
            pltpu.VMEM((H, NX * LR, DH), BF16),
            pltpu.VMEM((H, NX * OV, CW), BF16),
            pltpu.VMEM((H, NX, M, CW), BF16),
            pltpu.VMEM((H, NX, M, CW), BF16),
            pltpu.VMEM((M, CW), BF16),
            pltpu.VMEM((H, GR, CW), BF16),
            pltpu.VMEM((NZ, H, ROWS, CW), BF16),
            pltpu.VMEM((NY, H, ROWS, CW), BF16),
            pltpu.VMEM((SP, D), F32),
            pltpu.VMEM((NY, 8, ML), F32),
            pltpu.VMEM((8, ML), F32),
            pltpu.VMEM((NX, 8, ML), F32),
            pltpu.VMEM((NZ, 8, ML), F32),
            pltpu.VMEM((3, 8, ML), F32),
            dma,
            dma((H, NY)), dma((H, NY)), dma((H, NZ)), dma((H, NZ)),
            dma((H, NX)), dma((H, NX)), dma((H,)), dma((H,)),
            dma((H, 2)), dma((H, 2)), dma((H, NX)), dma((H, NX)),
            dma((H, NZ)), dma((H, NZ)), dma((H, NY)), dma((H, NY)),
            dma, dma, dma((NX,)), dma((NX,)), dma((NZ,)), dma((NZ,)), dma((NY,)), dma((NY,)),
        ],
        compiler_params=pltpu.CompilerParams(
            collective_id=0, has_side_effects=True, vmem_limit_bytes=60 << 20
        ),
        cost_estimate=pl.CostEstimate(
            flops=4 * M * V * D, bytes_accessed=2 * V * D, transcendentals=M * V
        ),
        name="readout",
    )(q, sc, gain, table, counts, positions)


def hand_out(a, b, out_a, out_b):
    out_a[...] = a[...]
    out_b[...] = b[...]


def on_device(quantized, scales, norm_gain, embed_table, counts, positions):
    expected, margins = readout(
        quantized[0], scales[0], norm_gain.reshape(1, D), embed_table, counts,
        positions.transpose(1, 2, 0),
    )
    vm = pl.BlockSpec(memory_space=pltpu.VMEM)
    expected, margins = pl.pallas_call(
        hand_out,
        out_shape=tuple(jax.ShapeDtypeStruct(a.shape, a.dtype) for a in (expected, margins)),
        in_specs=[vm, vm], out_specs=(vm, vm), name="hand_out",
    )(expected, margins)
    return (expected[None], margins)


def solution(mesh):
    in_specs = (
        P("vocab", None, "pos", None),
        P("vocab", None, "pos", None),
        P(),
        P("vocab", None),
        P(),
        P(None, None, "pos"),
    )
    out_specs = (P("vocab", None, "pos", None), P("pos", "vocab"))
    return jax.shard_map(
        on_device, mesh=mesh, in_specs=in_specs, out_specs=out_specs, check_vma=False
    )
```
